128 devices in a mesh: seq: 8 (over z, y_hi), expert: 16 (over y_lo, x, core).
Axes of the slice: x: 4, y: 4 (y_hi: 2, y_lo: 2; y = y_hi * 2 + y_lo), z: 4, core: 2. Of those that a mesh axis runs over, the one named last changes fastest.
Arguments:
- tokens: bfloat16 [131072, 1280], P(('seq', 'expert')), may hold values from -6 to 6
- slot_embed: bfloat16 [256, 1280], replicated, may hold values from -2 to 2
- w_in: bfloat16 [64, 1280, 3072], P('expert', None, 'seq'), may hold values from -0.15625 to 0.15625
- w_out: bfloat16 [64, 3072, 1280], P('expert', 'seq'), may hold values from -0.109375 to 0.109375
- cotangent: bfloat16 [131072, 1280], P(('seq', 'expert')), may hold values from -6 to 6
Outputs:
- token_grad: bfloat16 [131072, 1280], P(('seq', 'expert'))
- embed_grad: float32 [256, 1280], P(('seq', 'expert'))
- w_in_grad: bfloat16 [64, 1280, 3072], P('expert', None, 'seq')
- w_out_grad: bfloat16 [64, 3072, 1280], P('expert', 'seq')
The draws below stay inside these ranges and needn't reach their ends.
All inputs are finite; a program needn't handle non-finite values.
Results may differ from the reference program's by a relative error of at most 0.02.
Values may be sent and summed in bfloat16 or wider, within the bound.
A program may use at most 128 MiB of HBM per device.

```python
import jax
import jax.numpy as jnp
from jax import lax

D = 1280
FF = 3072
EXPERTS = 64
SLOT_EXP = 4
SLOTS = 256
TOKENS = 131072


def draw_tokens(key, part):
    key = jax.random.fold_in(key, 11)
    key_a, key_b = jax.random.split(key, 2)
    positions = jnp.arange(TOKENS, dtype=jnp.float32)[:, None]
    jitter = jnp.exp(jax.random.uniform(key_a, (TOKENS, 1), jnp.float32, -0.6, 0.6))
    scales = 0.5 * jnp.power(3.0, positions / TOKENS) * jitter
    result = jnp.clip(jax.random.normal(key_b, (TOKENS, D), jnp.float32) * scales, -6.0, 6.0)
    return result.astype(jnp.bfloat16)


def draw_slot_embed(key, part):
    key = jax.random.fold_in(key, 13)
    count = EXPERTS * SLOT_EXP
    result = jnp.clip(jax.random.normal(key, (count, D), jnp.float32), -6.0, 6.0) * D ** (-0.5)
    return result.astype(jnp.bfloat16)


def steps_of(rng, shape, shards, low, high):
    level = 1.0
    for axis_at, parts in shards:
        heights = jax.random.uniform(jax.random.fold_in(jax.random.fold_in(rng, 6), axis_at), (parts,), jnp.float32, low / len(shards), high / len(shards))
        level = level * jnp.repeat(jnp.exp(heights), shape[axis_at] // parts).reshape((-1,) + (1,) * (len(shape) - 1 - axis_at))
    return level


def gaussian(key, shape, scale, bound, cuts=(), kind=jnp.bfloat16):
    gain = steps_of(key, shape, cuts, -0.22, 0.18) if cuts else 1.0
    entries = jax.random.normal(key, shape, jnp.float32) * scale * gain
    return jnp.minimum(jnp.maximum(entries, -bound), bound).astype(kind)


def setup_inputs(seed: int = 0) -> dict:
    arg_keys = jax.random.split(jax.random.key(seed), 6)
    tokens = draw_tokens(jax.random.fold_in(arg_keys[5], 71), 0)
    slot_embed = draw_slot_embed(jax.random.fold_in(arg_keys[5], 71), 0)
    w_in = gaussian(arg_keys[2], (EXPERTS, D, FF), D ** -0.5, 0.15625, ((0, 16), (2, 8)))
    w_out = gaussian(arg_keys[3], (EXPERTS, FF, D), FF ** -0.5, 0.109375, ((0, 16), (1, 8)))
    cotangent = gaussian(arg_keys[4], (TOKENS, D), 1.0, 6.0, ((0, 128),))
    return dict(tokens=tokens, slot_embed=slot_embed, w_in=w_in, w_out=w_out, cotangent=cotangent)


def forward_one(item):
    slot_rows, first, second = item
    pre = jnp.dot(slot_rows, first, preferred_element_type=jnp.float32)
    hidden = jax.nn.gelu(pre, approximate=True).astype(jnp.bfloat16)
    result = jnp.dot(hidden, second, preferred_element_type=jnp.float32).astype(jnp.bfloat16)
    return (pre, hidden, result)

def backward_one(item):
    slot_rows, pre, hidden, grad_rows, first, second = item
    second_grad = jnp.dot(hidden.T, grad_rows, preferred_element_type=jnp.float32).astype(jnp.bfloat16)
    hid_grad = jnp.dot(grad_rows, second.T, preferred_element_type=jnp.float32)
    pre_grad = jax.vjp(lambda v: jax.nn.gelu(v, approximate=True), pre)[1](hid_grad)[0].astype(jnp.bfloat16)
    first_grad = jnp.dot(slot_rows.T, pre_grad, preferred_element_type=jnp.float32).astype(jnp.bfloat16)
    in_grad = jnp.dot(pre_grad, first.T, preferred_element_type=jnp.float32).astype(jnp.bfloat16)
    return (first_grad, second_grad, in_grad)

def reference(tokens, slot_embed, w_in, w_out, cotangent):
    logits = jnp.dot(tokens, slot_embed.T, preferred_element_type=jnp.float32)
    column_max = lax.optimization_barrier(jnp.max(logits, axis=0))
    raw_weights = jnp.exp(logits - column_max)
    dispatch_f = raw_weights / lax.optimization_barrier(jnp.sum(raw_weights, axis=0))
    dispatch = dispatch_f.astype(jnp.bfloat16)
    slot_in = jnp.dot(dispatch.T, tokens, preferred_element_type=jnp.float32).astype(jnp.bfloat16)
    grouped = slot_in.reshape(EXPERTS, SLOT_EXP, D)
    pre, hidden, slot_out = lax.map(forward_one, (grouped, w_in, w_out))
    slot_out = slot_out.reshape(SLOTS, D)
    combine_f = jax.nn.softmax(logits, axis=1)
    combine = combine_f.astype(jnp.bfloat16)
    slot_grad = jnp.dot(combine.T, cotangent, preferred_element_type=jnp.float32).astype(jnp.bfloat16)
    comb_grad = jnp.dot(cotangent, slot_out.T, preferred_element_type=jnp.float32)
    logit_comb = combine_f * (comb_grad - lax.optimization_barrier(jnp.sum(combine_f * comb_grad, axis=1, keepdims=True)))
    w_in_grad, w_out_grad, in_grad = lax.map(backward_one, (grouped, pre, hidden, slot_grad.reshape(EXPERTS, SLOT_EXP, D), w_in, w_out))
    in_grad = in_grad.reshape(SLOTS, D)
    disp_grad = jnp.dot(tokens, in_grad.T, preferred_element_type=jnp.float32)
    inner = lax.optimization_barrier(jnp.sum(dispatch_f * disp_grad, axis=0))
    logit_grad = (dispatch_f * (disp_grad - inner) + logit_comb).astype(jnp.bfloat16)
    token_grad = (jnp.dot(dispatch, in_grad, preferred_element_type=jnp.float32) + jnp.dot(logit_grad, slot_embed, preferred_element_type=jnp.float32)).astype(jnp.bfloat16)
    embed_grad = jnp.dot(logit_grad.T, tokens, preferred_element_type=jnp.float32)
    return (token_grad, embed_grad, w_in_grad, w_out_grad)
```

```python
import functools

import jax
import jax.numpy as jnp
from jax import lax
from jax.experimental import pallas as pl
from jax.experimental.pallas import tpu as pltpu
from jax.sharding import PartitionSpec as P

MESH = pl.DeviceIdType.MESH
F32 = jnp.float32
BF16 = jnp.bfloat16
CHUNK = 256
GELU_C = 0.7978845608028654
GELU_A = 0.044715


def coords():
    s = lax.axis_index("seq")
    e = lax.axis_index("expert")
    return s // 2, (s % 2) * 2 + e // 8, (e // 2) % 4, e % 2


def device(z, y, x, c):
    return (z * 2 + y // 2, (y % 2) * 8 + x * 2 + c)


def nn(a, b):
    return lax.dot_general(a, b, (((1,), (0,)), ((), ())), preferred_element_type=F32)


def nt(a, b):
    return lax.dot_general(a, b, (((1,), (1,)), ((), ())), preferred_element_type=F32)


def rows_at(start, size, unit):
    return pl.ds(pl.multiple_of(start, unit), size)


def split3(v):
    hi = v.astype(BF16).astype(F32)
    mid = (v - hi).astype(BF16).astype(F32)
    lo = (v - hi - mid).astype(BF16).astype(F32)
    return hi, mid, lo


def scalar_tile(columns):
    parts = [p for v in columns for p in split3(v)]
    rows = columns[0].shape[0]
    lane = lax.broadcasted_iota(jnp.int32, (rows, 128), 1)
    tile = jnp.zeros((rows, 128), F32)
    for i, p in enumerate(parts):
        tile = jnp.where((lane >= 16 * i) & (lane < 16 * i + 16), p, tile)
    return tile


def scalar_of(tile, i):
    a = 48 * i
    return tile[:, a : a + 1] + tile[:, a + 16 : a + 17] + tile[:, a + 32 : a + 33]


def chunk_tiles(v16, z):
    h, q = z // 2, z % 2
    return [v16[8 * h : 8 * h + 8, 640 * q + 128 * j : 640 * q + 128 * j + 128] for j in range(5)]


def unpack_rows(blocks):
    out = []
    for j in range(10):
        q, jj = j // 5, j % 5
        out.append(
            jnp.concatenate([blocks[q][8 * jj : 8 * jj + 8], blocks[2 + q][8 * jj : 8 * jj + 8]], axis=0)
        )
    return out


class Net:
    def __init__(self, ss, rs):
        self.ss, self.rs, self.count, self.all = ss, rs, 0, []

    def put(self, src, dst, dev):
        i = self.count
        self.count += 1
        copy = pltpu.make_async_remote_copy(
            src_ref=src, dst_ref=dst, send_sem=self.ss.at[i], recv_sem=self.rs.at[i],
            device_id=dev, device_id_type=MESH,
        )
        copy.start()
        self.all.append(copy)
        return copy


N_COPIES = 128
TILE0 = (8, 128)


def main_kernel(
    tok_h, emb_h, win_h, wout_h, cot_h,
    eg_o, lhs_o, rhs_o, sin_o, sgr_o, hid_o, pgr_o,
    tok, emb, win, wout, cot,
    lt, et, cf, cb, m_s, s_s,
    u_own, u_cs, u_cr, u_xs, u_xr, u_pk, u_yr, sall,
    g_own, g_cs, g_cr, g_pk, g_zr, g_pk2, g_yr, gall,
    o_pk, o_sr, oall, i_pk, i_sr, iall,
    l_all, inner_all,
    c_own, c_cs, c_cr, c_ys, c_yr, c_xs, c_xr, c_fs, c_fr,
    ld, ss, rs,
):
    z, y, x, c = coords()
    ylo, yhi = y % 2, y // 2
    oc = 1 - c
    D = tok.shape[1]
    net = Net(ss, rs)

    loads = {}

    def load(name, src, dst):
        cp = pltpu.make_async_copy(src, dst, ld.at[len(loads)])
        cp.start()
        loads[name] = cp

    for cc in range(2):
        for xx in range(4):
            for yy in range(2):
                g = yy * 8 + xx * 2 + cc
                p = cc * 128 + xx * 32 + yy * 16
                load(("emb", g), emb_h.at[pl.ds(16 * g, 16)], emb.at[pl.ds(p, 16)])
    n_chunks = tok.shape[0] // CHUNK
    for t in range(n_chunks):
        load(("tok", t), tok_h.at[pl.ds(t * CHUNK, CHUNK)], tok.at[pl.ds(t * CHUNK, CHUNK)])
    load("cot", cot_h, cot)
    load("win", win_h, win)
    load("wout", wout_h, wout)

    barrier = pltpu.get_barrier_semaphore()
    partners = [(z, y, x, oc)]
    partners += [((z + a) % 4, (y + b) % 4, x, c) for a in range(4) for b in range(4) if a or b]
    partners += [(z, (y + b) % 4, (x + a) % 4, c) for a in range(1, 4) for b in range(4)]
    for p in partners:
        pl.semaphore_signal(barrier, inc=1, device_id=device(*p), device_id_type=MESH)

    for g in range(16):
        loads[("emb", g)].wait()
    for t in range(n_chunks):
        loads[("tok", t)].wait()
        lt[:, t * CHUNK : (t + 1) * CHUNK] = nt(emb[...], tok[t * CHUNK : (t + 1) * CHUNK, :])

    @pl.loop(0, 8)
    def _(i):
        r = rows_at(i * 32, 32, 32)
        l = lt[r, :]
        m = jnp.max(l, axis=1, keepdims=True)
        e = jnp.exp(l - m)
        s = jnp.sum(e, axis=1, keepdims=True)
        et[r, :] = e.astype(BF16)
        m_s[r, :] = jnp.broadcast_to(m, (32, 128))
        s_s[r, :] = jnp.broadcast_to(s, (32, 128))

    ro = rows_at(oc * 128, 128, 128)
    rc = rows_at(c * 128, 128, 128)
    w_o = et[ro, :]
    for n in range(D // 256):
        u_cs[:, n * 256 : (n + 1) * 256] = nn(w_o, tok[:, n * 256 : (n + 1) * 256]).astype(BF16)
    u_cs[:, D : D + 128] = scalar_tile([m_s[ro, 0:1], s_s[ro, 0:1]]).astype(BF16)
    pl.semaphore_wait(barrier, len(partners))
    u_core = net.put(u_cs, u_cr, device(z, y, x, oc))
    w_c = et[rc, :]
    for n in range(D // 256):
        u_own[:, n * 256 : (n + 1) * 256] = nn(w_c, tok[:, n * 256 : (n + 1) * 256])

    @pl.loop(0, n_chunks)
    def _(t):
        k = rows_at(t * CHUNK, CHUNK, CHUNK)
        l = lt[:, k]
        e = jnp.exp(l - jnp.max(l, axis=0, keepdims=True))
        f = e / jnp.sum(e, axis=0, keepdims=True)
        cf[:, k] = f
        cb[:, k] = f.astype(BF16)

    u_core.wait_recv()

    @pl.loop(0, 8)
    def _(i):
        r = rows_at(i * 16, 16, 16)
        rg = rows_at(c * 128 + i * 16, 16, 16)
        v = u_cr[r, :].astype(F32)
        m1, s1 = m_s[rg, 0:1], s_s[rg, 0:1]
        sc = v[:, D : D + 128]
        m2, s2 = scalar_of(sc, 0), scalar_of(sc, 1)
        m = jnp.maximum(m1, m2)
        f1, f2 = jnp.exp(m1 - m), jnp.exp(m2 - m)
        s = s1 * f1 + s2 * f2
        u = u_own[r, :] * f1 + v[:, :D] * f2
        u_own[r, :] = u
        u_xs[r, :] = jnp.concatenate([u, scalar_tile([m, s])], axis=1).astype(BF16)
        m_s[rg, :] = jnp.broadcast_to(m, (16, 128))
        s_s[rg, :] = jnp.broadcast_to(s, (16, 128))

    u_x = []
    for k in range(1, 4):
        xx = (x + k) % 4
        u_x.append(net.put(u_xs.at[rows_at(xx * 32, 32, 32)], u_xr.at[k - 1], device(z, y, xx, c)))

    cot_load = loads["cot"]
    cot_load.wait()
    w_o = cb[ro, :]
    for n in range(D // 256):
        g_cs[:, n * 256 : (n + 1) * 256] = nn(w_o, cot[:, n * 256 : (n + 1) * 256]).astype(BF16)
    g_core = net.put(g_cs, g_cr, device(z, y, x, oc))
    w_c = cb[rc, :]
    for n in range(D // 256):
        g_own[:, n * 256 : (n + 1) * 256] = nn(w_c, cot[:, n * 256 : (n + 1) * 256])
    g_core.wait_recv()

    @pl.loop(0, 4)
    def _(i):
        r = rows_at(i * 32, 32, 32)
        v = g_own[r, :] + g_cr[r, :].astype(F32)
        for zz in range(4):
            tiles = chunk_tiles(v[:16], zz) + chunk_tiles(v[16:], zz)
            g_pk[zz, rows_at(i * 80, 80, 16), :] = jnp.concatenate(tiles, axis=0).astype(BF16)

    g_z = []
    for k in range(1, 4):
        zz = (z + k) % 4
        g_z.append(net.put(g_pk.at[zz], g_zr.at[k - 1], device(zz, y, x, c)))

    for cp in u_x:
        cp.wait_recv()
    for yy in range(2):
        r0 = x * 32 + yy * 16
        r = rows_at(r0, 16, 16)
        rg = rows_at(c * 128 + r0, 16, 16)
        ms, sums, us = [m_s[rg, 0:1]], [s_s[rg, 0:1]], [u_own[r, :]]
        for k in range(3):
            v = u_xr[k, yy * 16 : yy * 16 + 16, :].astype(F32)
            sc = v[:, D : D + 128]
            ms.append(scalar_of(sc, 0))
            sums.append(scalar_of(sc, 1))
            us.append(v[:, :D])
        m = functools.reduce(jnp.maximum, ms)
        fs = [jnp.exp(mk - m) for mk in ms]
        s = sum(a * f for a, f in zip(sums, fs))
        u = sum(a * f for a, f in zip(us, fs))
        for zz in range(4):
            h = zz // 2
            tile = scalar_tile([m[8 * h : 8 * h + 8], s[8 * h : 8 * h + 8]])
            u_pk[yy * 4 + zz] = jnp.concatenate(chunk_tiles(u, zz) + [tile], axis=0).astype(BF16)
    u_yz = []
    for a in range(4):
        for b in range(4):
            if a or b:
                zz, yy = (z + a) % 4, (y + b) % 4
                u_yz.append(net.put(u_pk.at[(yy % 2) * 4 + zz], u_yr.at[a * 4 + b], device(zz, yy, x, c)))
    u_yr[0] = u_pk[ylo * 4 + z]

    for cp in g_z:
        cp.wait_recv()

    @pl.loop(0, 4)
    def _(i):
        r = rows_at(i * 80, 80, 16)
        v = g_pk[z, r, :].astype(F32)
        for k in range(3):
            v = v + g_zr[k, r, :].astype(F32)
        pad = jnp.zeros(TILE0, F32)
        g_pk2[2 * i] = jnp.concatenate([v[:40], pad], axis=0).astype(BF16)
        g_pk2[2 * i + 1] = jnp.concatenate([v[40:], pad], axis=0).astype(BF16)

    g_xy = []
    for a in range(4):
        for b in range(4):
            if a or b:
                xx, yy = (x + a) % 4, (y + b) % 4
                g_xy.append(net.put(g_pk2.at[xx * 2 + yy % 2], g_yr.at[a * 4 + b], device(z, yy, xx, c)))
    g_yr[0] = g_pk2[x * 2 + ylo]

    for cp in u_yz:
        cp.wait_recv()
    parts = [u_yr[k].astype(F32) for k in range(16)]
    ms = [scalar_of(v[40:48], 0) for v in parts]
    sums = [scalar_of(v[40:48], 1) for v in parts]
    m = functools.reduce(jnp.maximum, ms)
    fs = [jnp.exp(mk - m) for mk in ms]
    s = sum(a * f for a, f in zip(sums, fs))
    lse = m + jnp.log(s)
    lse_tile = scalar_tile([lse])
    tiles = []
    for j in range(5):
        tiles.append(sum(v[8 * j : 8 * j + 8] * f for v, f in zip(parts, fs)) / s)
    sall[z] = jnp.concatenate(tiles + [lse_tile], axis=0).astype(BF16)
    u_ag = []
    for k in range(1, 4):
        u_ag.append(net.put(sall.at[z], sall.at[z], device((z + k) % 4, y, x, c)))
    loads["win"].wait()
    loads["wout"].wait()
    for cp in u_ag:
        cp.wait_recv()

    F = win.shape[2]
    expert_of = lax.broadcasted_iota(jnp.int32, (16, 1), 0) // 4
    slot_in = jnp.concatenate(unpack_rows([sall[k].astype(F32) for k in range(4)]), axis=1).astype(BF16)
    sin_o[...] = slot_in
    pre = jnp.zeros((16, F), F32)
    for e in range(4):
        pre = jnp.where(expert_of == e, nn(slot_in, win[e]), pre)
    th = jnp.tanh(GELU_C * (pre + GELU_A * pre * pre * pre))
    hidden_f = 0.5 * pre * (1.0 + th)
    slope = 0.5 * (1.0 + th) + 0.5 * pre * (1.0 - th * th) * GELU_C * (1.0 + 3.0 * GELU_A * pre * pre)
    hid_o[...] = hidden_f.astype(BF16)
    out_part = jnp.zeros((16, D), F32)
    for e in range(4):
        out_part += nn(jnp.where(expert_of == e, hidden_f, 0.0).astype(BF16), wout[e])
    pad = jnp.zeros(TILE0, F32)
    for zz in range(4):
        o_pk[zz] = jnp.concatenate(chunk_tiles(out_part, zz) + [pad], axis=0).astype(BF16)

    def seq_sums(pk, sr):
        cps = []
        for a in range(4):
            for b in range(2):
                if a or b:
                    zz = (z + a) % 4
                    cps.append(net.put(pk.at[zz], sr.at[a * 2 + b], device(zz, (y + 2 * b) % 4, x, c)))
        sr[0] = pk[z]
        return cps

    o_seq = seq_sums(o_pk, o_sr)

    for cp in g_xy:
        cp.wait_recv()
    acc = g_yr[0].astype(F32)
    for k in range(1, 16):
        acc = acc + g_yr[k].astype(F32)
    gall[z] = acc.astype(BF16)
    g_ag = []
    for k in range(1, 4):
        g_ag.append(net.put(gall.at[z], gall.at[z], device((z + k) % 4, y, x, c)))
    for cp in g_ag:
        cp.wait_recv()

    slot_grad = jnp.concatenate(unpack_rows([gall[k].astype(F32) for k in range(4)]), axis=1).astype(BF16)
    sgr_o[...] = slot_grad
    hid_grad = jnp.zeros((16, F), F32)
    for e in range(4):
        hid_grad = jnp.where(expert_of == e, nt(slot_grad, wout[e]), hid_grad)
    pre_grad = (hid_grad * slope).astype(BF16)
    pgr_o[...] = pre_grad
    in_part = jnp.zeros((16, D), F32)
    for e in range(4):
        in_part = jnp.where(expert_of == e, nt(pre_grad, win[e]), in_part)
    inner_part = jnp.sum(pre * pre_grad.astype(F32), axis=1, keepdims=True)
    for zz in range(4):
        h = zz // 2
        tile = scalar_tile([inner_part[8 * h : 8 * h + 8]])
        i_pk[zz] = jnp.concatenate(chunk_tiles(in_part, zz) + [tile], axis=0).astype(BF16)
    i_seq = seq_sums(i_pk, i_sr)

    for cp in o_seq:
        cp.wait_recv()
    acc = o_sr[0, 0:40, :].astype(F32)
    for k in range(1, 8):
        acc = acc + o_sr[k, 0:40, :].astype(F32)
    mine = c * 8 + x * 2 + ylo
    oall[mine, z] = jnp.concatenate([acc, lse_tile], axis=0).astype(BF16)
    o_1 = []
    for a in range(4):
        for b in range(2):
            if a or b:
                yy = y if b == 0 else yhi * 2 + 1 - ylo
                o_1.append(net.put(oall.at[mine, z], oall.at[mine, z], device((z + a) % 4, yy, x, c)))

    for cp in i_seq:
        cp.wait_recv()
    blocks = [i_sr[k].astype(F32) for k in range(8)]
    acc = sum(v[:40] for v in blocks)
    inner = sum(scalar_of(v[40:48], 0) for v in blocks)
    cz = c * 4 + z
    iall[cz, x * 2 + ylo] = jnp.concatenate([acc, scalar_tile([inner])], axis=0).astype(BF16)
    i_1 = []
    for a in range(4):
        for b in range(2):
            if a or b:
                yy = y if b == 0 else yhi * 2 + 1 - ylo
                ref = iall.at[cz, x * 2 + ylo]
                i_1.append(net.put(ref, ref, device(z, yy, (x + a) % 4, c)))

    for cp in o_1:
        cp.wait_recv()
    other = device(z, y, x, oc)
    o_2, o_3 = [], []
    ref = oall.at[pl.ds(c * 8 + x * 2, 2)]
    for k in range(1, 4):
        o_2.append(net.put(ref, ref, device(z, y, (x + k) % 4, c)))
    o_3.append(net.put(ref, ref, other))
    for cp in i_1:
        cp.wait_recv()
    i_2, i_3 = [], []
    ref = iall.at[cz]
    for k in range(1, 4):
        i_2.append(net.put(ref, ref, device((z + k) % 4, y, x, c)))
    i_3.append(net.put(ref, ref, other))
    for k in range(1, 4):
        o_2[k - 1].wait_recv()
        ref = oall.at[pl.ds(c * 8 + ((x - k + 4) % 4) * 2, 2)]
        o_3.append(net.put(ref, ref, other))
    for k in range(1, 4):
        i_2[k - 1].wait_recv()
        ref = iall.at[c * 4 + (z - k + 4) % 4]
        i_3.append(net.put(ref, ref, other))
    for cp in o_3:
        cp.wait_recv()

    half = rhs_o.shape[0] // 2

    @pl.loop(0, 16)
    def _(i):
        blocks = [oall[i, k].astype(F32) for k in range(4)]
        r = rows_at(i * 16, 16, 16)
        for j, t in enumerate(unpack_rows(blocks)):
            rhs_o[r, j * 128 : (j + 1) * 128] = t.astype(BF16)
        lse16 = jnp.concatenate([scalar_of(blocks[0][40:48], 0), scalar_of(blocks[2][40:48], 0)], axis=0)
        l_all[r, :] = jnp.broadcast_to(lse16, (16, 128))

    @pl.loop(0, n_chunks)
    def _(t):
        k = rows_at(t * CHUNK, CHUNK, CHUNK)
        cg = nt(rhs_o[0:half, :], cot[k, :])
        f = cf[:, k]
        cf[:, k] = f * (cg - jnp.sum(f * cg, axis=0, keepdims=True))

    for cp in i_3:
        cp.wait_recv()

    @pl.loop(0, 16)
    def _(i):
        cc, kk = i // 8, i % 8
        blocks = [iall[cc * 4 + k, kk].astype(F32) for k in range(4)]
        r = rows_at(i * 16, 16, 16)
        for j, t in enumerate(unpack_rows(blocks)):
            rhs_o[r, j * 128 : (j + 1) * 128] = t.astype(BF16)
        in16 = jnp.concatenate([scalar_of(blocks[0][40:48], 0), scalar_of(blocks[2][40:48], 0)], axis=0)
        inner_all[r, :] = jnp.broadcast_to(in16, (16, 128))

    rhs_o[half:, :] = emb[...]

    @pl.loop(0, n_chunks)
    def _(t):
        k = rows_at(t * CHUNK, CHUNK, CHUNK)
        dg = nt(rhs_o[0:half, :], tok[k, :])
        df = jnp.exp(lt[:, k] - l_all[:, 0:1])
        lhs_o[0:half, k] = df.astype(BF16)
        lhs_o[half:, k] = (df * (dg - inner_all[:, 0:1]) + cf[:, k]).astype(BF16)

    H = D // 2
    for a, b in ((0, 256), (256, 256), (512, 128)):
        w = tok[:, rows_at(oc * H + a, b, 128)]
        c_cs[:, a : a + b] = nn(lhs_o[half:, :], w).astype(BF16)
    c_core = net.put(c_cs, c_cr, other)
    for a, b in ((0, 256), (256, 256), (512, 128)):
        w = tok[:, rows_at(c * H + a, b, 128)]
        c_own[:, a : a + b] = nn(lhs_o[half:, :], w)
    c_core.wait_recv()

    @pl.loop(0, 16)
    def _(i):
        r = rows_at(i * 16, 16, 16)
        c_ys[r, :] = (c_own[r, :] + c_cr[r, :].astype(F32)).astype(BF16)

    def block_of(zz, yy):
        return rows_at((yy % 2) * 128 + ((zz % 2) * 2 + yy // 2) * 32 + (zz // 2) * 16, 16, 16)

    c_y = []
    for a in range(4):
        for b in range(4):
            if a or b:
                zz, yy = (z + a) % 4, (y + b) % 4
                c_y.append(net.put(c_ys.at[block_of(zz, yy)], c_yr.at[a * 4 + b], device(zz, yy, x, c)))
    c_yr[0] = c_ys[block_of(z, y), :]
    for cp in c_y:
        cp.wait_recv()
    acc = c_yr[0].astype(F32)
    for k in range(1, 16):
        acc = acc + c_yr[k].astype(F32)
    c_xs[...] = acc
    c_x = []
    for k in range(1, 4):
        c_x.append(net.put(c_xs, c_xr.at[k - 1], device(z, y, (x + k) % 4, c)))
    for cp in c_x:
        cp.wait_recv()
    c_fs[...] = c_xs[...] + c_xr[0] + c_xr[1] + c_xr[2]
    c_f = net.put(c_fs, c_fr, other)

    def my_rows(ref):
        v = ref[rows_at((x // 2) * 8, 8, 8), :]
        k = (x % 2) * 2 + c
        out = v[0:2]
        for i in range(1, 4):
            out = jnp.where(k == i, v[2 * i : 2 * i + 2], out)
        return out

    eg_o[:, rows_at(c * H, H, 128)] = my_rows(c_fs)
    c_f.wait_recv()
    eg_o[:, rows_at(oc * H, H, 128)] = my_rows(c_fr)

    for cp in net.all:
        cp.wait_send()


def on_device(tokens, slot_embed, w_in, w_out, cotangent):
    T, D = tokens.shape
    S = slot_embed.shape[0]
    E, _, F = w_in.shape
    V = pltpu.VMEM
    shape = jax.ShapeDtypeStruct
    blk = (48, 128)
    scratch = [
        V((T, D), BF16), V((S, D), BF16), V(w_in.shape, BF16), V(w_out.shape, BF16), V((T, D), BF16),
        V((S, T), F32), V((S, T), BF16), V((S, T), F32), V((S, T), BF16), V((S, 128), F32), V((S, 128), F32),
        V((128, D), F32), V((128, D + 128), BF16), V((128, D + 128), BF16),
        V((128, D + 128), BF16), V((3, 32, D + 128), BF16), V((8,) + blk, BF16), V((16,) + blk, BF16), V((4,) + blk, BF16),
        V((128, D), F32), V((128, D), BF16), V((128, D), BF16), V((4, 320, 128), BF16), V((3, 320, 128), BF16),
        V((8,) + blk, BF16), V((16,) + blk, BF16), V((4,) + blk, BF16),
        V((4,) + blk, BF16), V((8,) + blk, BF16), V((16, 4) + blk, BF16),
        V((4,) + blk, BF16), V((8,) + blk, BF16), V((8, 8) + blk, BF16),
        V((S, 128), F32), V((S, 128), F32),
        V((S, D // 2), F32), V((S, D // 2), BF16), V((S, D // 2), BF16), V((S, D // 2), BF16),
        V((16, 16, D // 2), BF16), V((16, D // 2), F32), V((3, 16, D // 2), F32), V((16, D // 2), F32), V((16, D // 2), F32),
        pltpu.SemaphoreType.DMA((32,)),
        pltpu.SemaphoreType.DMA((N_COPIES,)),
        pltpu.SemaphoreType.DMA((N_COPIES,)),
    ]
    eg, lhs, rhs, slot_in, slot_grad, hidden, pre_grad = pl.pallas_call(
        main_kernel,
        name="moe_exchange",
        out_shape=[
            shape((2, D), F32), shape((2 * S, T), BF16), shape((2 * S, D), BF16),
            shape((16, D), BF16), shape((16, D), BF16), shape((16, F), BF16), shape((16, F), BF16),
        ],
        in_specs=[pl.BlockSpec(memory_space=pl.ANY)] * 5,
        out_specs=[pl.BlockSpec(memory_space=pltpu.VMEM)] * 7,
        scratch_shapes=scratch,
        compiler_params=pltpu.CompilerParams(
            collective_id=0, has_side_effects=True, vmem_limit_bytes=60 * 2**20
        ),
    )(tokens, slot_embed, w_in, w_out, cotangent)
    token_grad = lax.dot_general(lhs, rhs, (((0,), (0,)), ((), ())), preferred_element_type=F32).astype(BF16)

    def grouped(v):
        return v.reshape(E, -1, v.shape[1])

    w_out_grad = jnp.einsum(
        "esf,esd->efd", grouped(hidden), grouped(slot_grad), preferred_element_type=F32
    ).astype(BF16)
    w_in_grad = jnp.einsum(
        "esd,esf->edf", grouped(slot_in), grouped(pre_grad), preferred_element_type=F32
    ).astype(BF16)
    return (token_grad, eg, w_in_grad, w_out_grad)


def solution(mesh):
    in_specs = (
        P(("seq", "expert"), None),
        P(),
        P("expert", None, "seq"),
        P("expert", "seq", None),
        P(("seq", "expert"), None),
    )
    out_specs = (
        P(("seq", "expert"), None),
        P(("seq", "expert"), None),
        P("expert", None, "seq"),
        P("expert", "seq", None),
    )
    return jax.shard_map(
        on_device, mesh=mesh, in_specs=in_specs, out_specs=out_specs, check_vma=False
    )
```

```python
import functools

import jax
import jax.numpy as jnp
from jax import lax
from jax.experimental import pallas as pl
from jax.experimental.pallas import tpu as pltpu
from jax.sharding import PartitionSpec as P

MESH = pl.DeviceIdType.MESH
F32 = jnp.float32
BF16 = jnp.bfloat16
CHUNK = 256
GELU_C = 0.7978845608028654
GELU_A = 0.044715


def coords():
    s = lax.axis_index("seq")
    e = lax.axis_index("expert")
    return s // 2, (s % 2) * 2 + e // 8, (e // 2) % 4, e % 2


def device(z, y, x, c):
    return (z * 2 + y // 2, (y % 2) * 8 + x * 2 + c)


def nn(a, b):
    return lax.dot_general(a, b, (((1,), (0,)), ((), ())), preferred_element_type=F32)


def nt(a, b):
    return lax.dot_general(a, b, (((1,), (1,)), ((), ())), preferred_element_type=F32)


def rows_at(start, size, unit):
    return pl.ds(pl.multiple_of(start, unit), size)


def split3(v):
    hi = v.astype(BF16).astype(F32)
    mid = (v - hi).astype(BF16).astype(F32)
    lo = (v - hi - mid).astype(BF16).astype(F32)
    return hi, mid, lo


def scalar_tile(columns):
    parts = [p for v in columns for p in split3(v)]
    rows = columns[0].shape[0]
    lane = lax.broadcasted_iota(jnp.int32, (rows, 128), 1)
    tile = jnp.zeros((rows, 128), F32)
    for i, p in enumerate(parts):
        tile = jnp.where((lane >= 16 * i) & (lane < 16 * i + 16), p, tile)
    return tile


def scalar_of(tile, i):
    a = 48 * i
    return tile[:, a : a + 1] + tile[:, a + 16 : a + 17] + tile[:, a + 32 : a + 33]


def chunk_tiles(v16, z):
    h, q = z // 2, z % 2
    return [v16[8 * h : 8 * h + 8, 640 * q + 128 * j : 640 * q + 128 * j + 128] for j in range(5)]


def unpack_rows(blocks):
    out = []
    for j in range(10):
        q, jj = j // 5, j % 5
        out.append(
            jnp.concatenate([blocks[q][8 * jj : 8 * jj + 8], blocks[2 + q][8 * jj : 8 * jj + 8]], axis=0)
        )
    return out


class Group:
    def __init__(self, net, index, total):
        self.net, self.index, self.total = net, index, total

    def copy(self, src, dst, dev):
        return pltpu.make_async_remote_copy(
            src_ref=src, dst_ref=dst, send_sem=self.net.ss.at[self.index], recv_sem=self.net.rs.at[self.index],
            device_id=dev, device_id_type=MESH,
        )

    def put(self, src, dst, dev):
        self.copy(src, dst, dev).start()

    def wait_recv(self):
        self.copy(self.total, self.total, self.net.other).wait_recv()

    def wait_send(self):
        self.copy(self.total, self.total, self.net.other).wait_send()


class Net:
    def __init__(self, ss, rs, other):
        self.ss, self.rs, self.other, self.groups = ss, rs, other, []

    def group(self, total):
        g = Group(self, len(self.groups), total)
        self.groups.append(g)
        return g

    def put(self, src, dst, dev):
        g = self.group(dst)
        g.put(src, dst, dev)
        return g


N_GROUPS = 29
TILE0 = (8, 128)


def main_kernel(
    tok_h, emb_h, win_h, wout_h, cot_h,
    eg_o, lhs_o, rhs_o, sin_o, sgr_o, hid_o, pgr_o,
    tok, emb, win, wout, cot,
    lt, et, cf, cb, m_s, s_s,
    u_own, u_cs, u_cr, u_xs, u_xr, u_pk, u_yr, sall,
    g_own, g_cs, g_cr, g_pk, g_zr, g_pk2, g_yr, gall,
    o_pk, o_sr, oall, i_pk, i_sr, iall,
    l_all, inner_all,
    c_own, c_cs, c_cr, c_ys, c_yr, c_xs, c_xr,
    ld, ss, rs,
):
    z, y, x, c = coords()
    ylo, yhi = y % 2, y // 2
    oc = 1 - c
    D = tok.shape[1]
    other = device(z, y, x, oc)
    net = Net(ss, rs, other)

    loads = {}

    def load(name, src, dst):
        cp = pltpu.make_async_copy(src, dst, ld.at[len(loads)])
        cp.start()
        loads[name] = cp

    for cc in range(2):
        for xx in range(4):
            for yy in range(2):
                g = yy * 8 + xx * 2 + cc
                p = cc * 128 + xx * 32 + yy * 16
                pltpu.make_async_copy(emb_h.at[pl.ds(16 * g, 16)], emb.at[pl.ds(p, 16)], ld.at[0]).start()
    loads["emb"] = pltpu.make_async_copy(emb_h, emb, ld.at[0])
    n_chunks = tok.shape[0] // CHUNK
    for t in range(n_chunks):
        load(("tok", t), tok_h.at[pl.ds(t * CHUNK, CHUNK)], tok.at[pl.ds(t * CHUNK, CHUNK)])
    load("cot", cot_h, cot)
    load("win", win_h, win)
    load("wout", wout_h, wout)

    barrier = pltpu.get_barrier_semaphore()
    partners = [(z, y, x, oc)]
    partners += [((z + a) % 4, (y + b) % 4, x, c) for a in range(4) for b in range(4) if a or b]
    partners += [(z, (y + b) % 4, (x + a) % 4, c) for a in range(1, 4) for b in range(4)]
    partners += [(z, y, (x + a) % 4, oc) for a in range(1, 4)]
    for p in partners:
        pl.semaphore_signal(barrier, inc=1, device_id=device(*p), device_id_type=MESH)

    loads["emb"].wait()
    for t in range(n_chunks):
        loads[("tok", t)].wait()
        lt[:, t * CHUNK : (t + 1) * CHUNK] = nt(emb[...], tok[t * CHUNK : (t + 1) * CHUNK, :])

    @pl.loop(0, 8, unroll=4)
    def _(i):
        r = rows_at(i * 32, 32, 32)
        l = lt[r, :]
        m = jnp.max(l, axis=1, keepdims=True)
        e = jnp.exp(l - m)
        s = jnp.sum(e, axis=1, keepdims=True)
        et[r, :] = e.astype(BF16)
        m_s[r, :] = jnp.broadcast_to(m, (32, 128))
        s_s[r, :] = jnp.broadcast_to(s, (32, 128))

    ro = rows_at(oc * 128, 128, 128)
    rc = rows_at(c * 128, 128, 128)
    w_o = et[ro, :]
    for n in range(D // 256):
        u_cs[:, n * 256 : (n + 1) * 256] = nn(w_o, tok[:, n * 256 : (n + 1) * 256]).astype(BF16)
    u_cs[:, D : D + 128] = scalar_tile([m_s[ro, 0:1], s_s[ro, 0:1]]).astype(BF16)
    pl.semaphore_wait(barrier, len(partners))
    u_core = net.put(u_cs, u_cr, device(z, y, x, oc))
    w_c = et[rc, :]
    for n in range(D // 256):
        u_own[:, n * 256 : (n + 1) * 256] = nn(w_c, tok[:, n * 256 : (n + 1) * 256])

    @pl.loop(0, n_chunks)
    def _(t):
        k = rows_at(t * CHUNK, CHUNK, CHUNK)
        l = lt[:, k]
        e = jnp.exp(l - jnp.max(l, axis=0, keepdims=True))
        f = e / jnp.sum(e, axis=0, keepdims=True)
        cf[:, k] = f
        cb[:, k] = f.astype(BF16)

    u_core.wait_recv()

    @pl.loop(0, 8, unroll=4)
    def _(i):
        r = rows_at(i * 16, 16, 16)
        rg = rows_at(c * 128 + i * 16, 16, 16)
        v = u_cr[r, :].astype(F32)
        m1, s1 = m_s[rg, 0:1], s_s[rg, 0:1]
        sc = v[:, D : D + 128]
        m2, s2 = scalar_of(sc, 0), scalar_of(sc, 1)
        m = jnp.maximum(m1, m2)
        f1, f2 = jnp.exp(m1 - m), jnp.exp(m2 - m)
        s = s1 * f1 + s2 * f2
        u = u_own[r, :] * f1 + v[:, :D] * f2
        u_own[r, :] = u
        u_xs[r, :] = jnp.concatenate([u, scalar_tile([m, s])], axis=1).astype(BF16)
        m_s[rg, :] = jnp.broadcast_to(m, (16, 128))
        s_s[rg, :] = jnp.broadcast_to(s, (16, 128))

    u_x = net.group(u_xr)
    for k in range(1, 4):
        xx = (x + k) % 4
        u_x.put(u_xs.at[rows_at(xx * 32, 32, 32)], u_xr.at[k - 1], device(z, y, xx, c))

    cot_load = loads["cot"]
    cot_load.wait()
    w_o = cb[ro, :]
    for n in range(D // 256):
        g_cs[:, n * 256 : (n + 1) * 256] = nn(w_o, cot[:, n * 256 : (n + 1) * 256]).astype(BF16)
    g_core = net.put(g_cs, g_cr, device(z, y, x, oc))
    w_c = cb[rc, :]
    for n in range(D // 256):
        g_own[:, n * 256 : (n + 1) * 256] = nn(w_c, cot[:, n * 256 : (n + 1) * 256])
    g_core.wait_recv()

    @pl.loop(0, 4, unroll=2)
    def _(i):
        r = rows_at(i * 32, 32, 32)
        v = g_own[r, :] + g_cr[r, :].astype(F32)
        for zz in range(4):
            tiles = chunk_tiles(v[:16], zz) + chunk_tiles(v[16:], zz)
            g_pk[zz, rows_at(i * 80, 80, 16), :] = jnp.concatenate(tiles, axis=0).astype(BF16)

    g_z = net.group(g_zr)
    for k in range(1, 4):
        zz = (z + k) % 4
        g_z.put(g_pk.at[zz], g_zr.at[k - 1], device(zz, y, x, c))

    u_x.wait_recv()
    for yy in range(2):
        r0 = x * 32 + yy * 16
        r = rows_at(r0, 16, 16)
        rg = rows_at(c * 128 + r0, 16, 16)
        ms, sums, us = [m_s[rg, 0:1]], [s_s[rg, 0:1]], [u_own[r, :]]
        for k in range(3):
            v = u_xr[k, yy * 16 : yy * 16 + 16, :].astype(F32)
            sc = v[:, D : D + 128]
            ms.append(scalar_of(sc, 0))
            sums.append(scalar_of(sc, 1))
            us.append(v[:, :D])
        m = functools.reduce(jnp.maximum, ms)
        fs = [jnp.exp(mk - m) for mk in ms]
        s = sum(a * f for a, f in zip(sums, fs))
        u = sum(a * f for a, f in zip(us, fs))
        for zz in range(4):
            h = zz // 2
            tile = scalar_tile([m[8 * h : 8 * h + 8], s[8 * h : 8 * h + 8]])
            u_pk[yy * 4 + zz] = jnp.concatenate(chunk_tiles(u, zz) + [tile], axis=0).astype(BF16)
    u_yz = net.group(u_yr.at[pl.ds(1, 15)])
    for a in range(4):
        for b in range(4):
            if a or b:
                zz, yy = (z + a) % 4, (y + b) % 4
                u_yz.put(u_pk.at[(yy % 2) * 4 + zz], u_yr.at[a * 4 + b], device(zz, yy, x, c))
    u_yr[0] = u_pk[ylo * 4 + z]

    g_z.wait_recv()

    @pl.loop(0, 4, unroll=2)
    def _(i):
        r = rows_at(i * 80, 80, 16)
        v = g_pk[z, r, :].astype(F32)
        for k in range(3):
            v = v + g_zr[k, r, :].astype(F32)
        pad = jnp.zeros(TILE0, F32)
        g_pk2[2 * i] = jnp.concatenate([v[:40], pad], axis=0).astype(BF16)
        g_pk2[2 * i + 1] = jnp.concatenate([v[40:], pad], axis=0).astype(BF16)

    g_xy = net.group(g_yr.at[pl.ds(1, 15)])
    for a in range(4):
        for b in range(4):
            if a or b:
                xx, yy = (x + a) % 4, (y + b) % 4
                g_xy.put(g_pk2.at[xx * 2 + yy % 2], g_yr.at[a * 4 + b], device(z, yy, xx, c))
    g_yr[0] = g_pk2[x * 2 + ylo]

    u_yz.wait_recv()
    parts = [u_yr[k].astype(F32) for k in range(16)]
    ms = [scalar_of(v[40:48], 0) for v in parts]
    sums = [scalar_of(v[40:48], 1) for v in parts]
    m = functools.reduce(jnp.maximum, ms)
    fs = [jnp.exp(mk - m) for mk in ms]
    s = sum(a * f for a, f in zip(sums, fs))
    lse = m + jnp.log(s)
    lse_tile = scalar_tile([lse])
    tiles = []
    for j in range(5):
        tiles.append(sum(v[8 * j : 8 * j + 8] * f for v, f in zip(parts, fs)) / s)
    sall[z] = jnp.concatenate(tiles + [lse_tile], axis=0).astype(BF16)
    u_ag = net.group(sall.at[pl.ds(0, 3)])
    for k in range(1, 4):
        u_ag.put(sall.at[z], sall.at[z], device((z + k) % 4, y, x, c))

    g_xy.wait_recv()
    acc = g_yr[0].astype(F32)
    for k in range(1, 16):
        acc = acc + g_yr[k].astype(F32)
    gall[z] = acc.astype(BF16)
    g_ag = net.group(gall.at[pl.ds(0, 3)])
    for k in range(1, 4):
        g_ag.put(gall.at[z], gall.at[z], device((z + k) % 4, y, x, c))
    loads["win"].wait()
    loads["wout"].wait()
    u_ag.wait_recv()

    F = win.shape[2]
    expert_of = lax.broadcasted_iota(jnp.int32, (16, 1), 0) // 4
    slot_in = jnp.concatenate(unpack_rows([sall[k].astype(F32) for k in range(4)]), axis=1).astype(BF16)
    sin_o[...] = slot_in
    pre = jnp.zeros((16, F), F32)
    for e in range(4):
        pre = jnp.where(expert_of == e, nn(slot_in, win[e]), pre)
    th = jnp.tanh(GELU_C * (pre + GELU_A * pre * pre * pre))
    hidden_f = 0.5 * pre * (1.0 + th)
    slope = 0.5 * (1.0 + th) + 0.5 * pre * (1.0 - th * th) * GELU_C * (1.0 + 3.0 * GELU_A * pre * pre)
    hid_o[...] = hidden_f.astype(BF16)
    out_part = jnp.zeros((16, D), F32)
    for e in range(4):
        out_part += nn(jnp.where(expert_of == e, hidden_f, 0.0).astype(BF16), wout[e])
    for zz in range(4):
        tile = sall[zz, 40:48, :].astype(F32)
        o_pk[zz] = jnp.concatenate(chunk_tiles(out_part, zz) + [tile], axis=0).astype(BF16)

    def seq_sums(pk, sr):
        group = net.group(sr.at[pl.ds(1, 15)])
        for a in range(4):
            for b in range(4):
                if a or b:
                    zz = (z + a) % 4
                    group.put(pk.at[zz], sr.at[a * 4 + b], device(zz, (y + b) % 4, x, c))
        sr[0] = pk[z]
        return group

    def seq_total(sr, parity, rows):
        ks = [a * 4 + b for a in range(4) for b in range(4) if b % 2 == parity]
        acc = sr[ks[0], 0:rows, :].astype(F32)
        for k in ks[1:]:
            acc = acc + sr[k, 0:rows, :].astype(F32)
        return acc

    o_seq = seq_sums(o_pk, o_sr)

    g_ag.wait_recv()

    slot_grad = jnp.concatenate(unpack_rows([gall[k].astype(F32) for k in range(4)]), axis=1).astype(BF16)
    sgr_o[...] = slot_grad
    hid_grad = jnp.zeros((16, F), F32)
    for e in range(4):
        hid_grad = jnp.where(expert_of == e, nt(slot_grad, wout[e]), hid_grad)
    pre_grad = (hid_grad * slope).astype(BF16)
    pgr_o[...] = pre_grad
    in_part = jnp.zeros((16, D), F32)
    for e in range(4):
        in_part = jnp.where(expert_of == e, nt(pre_grad, win[e]), in_part)
    inner_part = jnp.sum(pre * pre_grad.astype(F32), axis=1, keepdims=True)
    for zz in range(4):
        h = zz // 2
        tile = scalar_tile([inner_part[8 * h : 8 * h + 8]])
        i_pk[zz] = jnp.concatenate(chunk_tiles(in_part, zz) + [tile], axis=0).astype(BF16)
    i_seq = seq_sums(i_pk, i_sr)

    o_seq.wait_recv()
    pair = c * 8 + x * 2
    for parity in range(2):
        acc = seq_total(o_sr, parity, 40)
        lse_tile = o_sr[parity, 40:48, :].astype(F32)
        oall[pair + (ylo + parity) % 2, z] = jnp.concatenate([acc, lse_tile], axis=0).astype(BF16)
    o_1 = net.group(oall.at[pl.ds(0, 2), pl.ds(0, 3)])
    for k in range(1, 4):
        ref = oall.at[pl.ds(pair, 2), z]
        o_1.put(ref, ref, device((z + k) % 4, y, x, c))

    i_seq.wait_recv()
    cz = c * 4 + z
    for parity in range(2):
        acc = seq_total(i_sr, parity, 48)
        inner = scalar_of(acc[40:48], 0)
        block = jnp.concatenate([acc[:40], scalar_tile([inner])], axis=0)
        iall[cz, x * 2 + (ylo + parity) % 2] = block.astype(BF16)
    i_1 = net.group(iall.at[0, pl.ds(0, 6)])
    for k in range(1, 4):
        ref = iall.at[cz, pl.ds(x * 2, 2)]
        i_1.put(ref, ref, device(z, y, (x + k) % 4, c))

    half = rhs_o.shape[0] // 2

    def place(i, blocks, scalars):
        r = rows_at(i * 16, 16, 16)
        for j, t in enumerate(unpack_rows(blocks)):
            rhs_o[r, j * 128 : (j + 1) * 128] = t.astype(BF16)
        v = jnp.concatenate([scalar_of(blocks[0][40:48], 0), scalar_of(blocks[2][40:48], 0)], axis=0)
        scalars[r, :] = jnp.broadcast_to(v, (16, 128))

    def place_out(first):
        for i in range(2):
            place(first + i, [oall[first + i, k].astype(F32) for k in range(4)], l_all)

    def place_in(core):
        @pl.loop(0, 8, unroll=4)
        def _(k):
            place(core * 8 + k, [iall[core * 4 + zz, k].astype(F32) for zz in range(4)], inner_all)

    o_1.wait_recv()
    o_2, o_3 = [], []
    ref = oall.at[pl.ds(pair, 2)]
    for k in range(1, 4):
        o_2.append(net.put(ref, ref, device(z, y, (x + k) % 4, c)))
    o_3.append(net.put(ref, ref, other))
    place_out(pair)
    i_1.wait_recv()
    i_2, i_3 = [], []
    ref = iall.at[cz]
    for k in range(1, 4):
        i_2.append(net.put(ref, ref, device((z + k) % 4, y, x, c)))
    i_3.append(net.put(ref, ref, other))
    for k in range(1, 4):
        o_2[k - 1].wait_recv()
        first = c * 8 + ((x - k + 4) % 4) * 2
        ref = oall.at[pl.ds(first, 2)]
        o_3.append(net.put(ref, ref, other))
        place_out(first)
    for k in range(4):
        o_3[k].wait_recv()
        place_out(oc * 8 + ((x - k + 4) % 4) * 2)
    for k in range(1, 4):
        i_2[k - 1].wait_recv()
        ref = iall.at[c * 4 + (z - k + 4) % 4]
        i_3.append(net.put(ref, ref, other))

    @pl.loop(0, n_chunks)
    def _(t):
        k = rows_at(t * CHUNK, CHUNK, CHUNK)
        cg = nt(rhs_o[0:half, :], cot[k, :])
        f = cf[:, k]
        cf[:, k] = f * (cg - jnp.sum(f * cg, axis=0, keepdims=True))

    place_in(c)
    for cp in i_3:
        cp.wait_recv()
    place_in(oc)
    rhs_o[half:, :] = emb[...]

    @pl.loop(0, n_chunks)
    def _(t):
        k = rows_at(t * CHUNK, CHUNK, CHUNK)
        dg = nt(rhs_o[0:half, :], tok[k, :])
        df = jnp.exp(lt[:, k] - l_all[:, 0:1])
        lhs_o[0:half, k] = df.astype(BF16)
        lhs_o[half:, k] = (df * (dg - inner_all[:, 0:1]) + cf[:, k]).astype(BF16)

    H = D // 2
    pieces = ((0, 384), (384, 256))
    c_core = net.group(c_cr)
    for a, b in pieces:
        c_cs[:, a : a + b] = nn(lhs_o[half:, :], tok[:, rows_at(oc * H + a, b, 128)]).astype(BF16)
        c_core.put(c_cs.at[:, a : a + b], c_cr.at[:, a : a + b], other)
    for a, b in pieces:
        c_own[:, a : a + b] = nn(lhs_o[half:, :], tok[:, rows_at(c * H + a, b, 128)])
    c_core.wait_recv()

    @pl.loop(0, 16, unroll=4)
    def _(i):
        r = rows_at(i * 16, 16, 16)
        c_ys[r, :] = (c_own[r, :] + c_cr[r, :].astype(F32)).astype(BF16)

    def block_of(zz, yy):
        return rows_at((yy % 2) * 128 + ((zz % 2) * 2 + yy // 2) * 32 + (zz // 2) * 16, 16, 16)

    c_y = net.group(c_yr.at[pl.ds(1, 15)])
    for a in range(4):
        for b in range(4):
            if a or b:
                zz, yy = (z + a) % 4, (y + b) % 4
                c_y.put(c_ys.at[block_of(zz, yy)], c_yr.at[a * 4 + b], device(zz, yy, x, c))
    c_yr[0] = c_ys[block_of(z, y), :]
    c_y.wait_recv()
    acc = c_yr[0].astype(F32)
    for k in range(1, 16):
        acc = acc + c_yr[k].astype(F32)
    c_xs[0] = acc[0:8]
    c_xs[1] = acc[8:16]
    c_x = net.group(c_xr.at[pl.ds(1, 7)])
    for k in range(4):
        for d in range(2):
            if k or d:
                xx, cc = (x + k) % 4, c if d == 0 else oc
                c_x.put(c_xs.at[xx // 2], c_xr.at[k * 2 + d], device(z, y, xx, cc))
    c_xr[0] = c_xs[x // 2]
    c_x.wait_recv()
    for d in range(2):
        v = c_xr[d] + c_xr[2 + d] + c_xr[4 + d] + c_xr[6 + d]
        k = (x % 2) * 2 + c
        out = v[0:2]
        for i in range(1, 4):
            out = jnp.where(k == i, v[2 * i : 2 * i + 2], out)
        eg_o[:, rows_at((c if d == 0 else oc) * H, H, 128)] = out

    for g in net.groups:
        g.wait_send()


def tn(a, b):
    return lax.dot_general(a, b, (((0,), (0,)), ((), ())), preferred_element_type=F32)


def grads_kernel(eg, lhs, rhs, sin, sgr, hid, pgr, eg_h, tg_h, wi_h, wo_h, tg, wi, wo, sem):
    copies = []

    def store(src, dst):
        cp = pltpu.make_async_copy(src, dst, sem.at[len(copies)])
        cp.start()
        copies.append(cp)

    store(eg, eg_h)
    expert_of = lax.broadcasted_iota(jnp.int32, (16, 1), 0) // 4
    for e in range(wo.shape[0]):
        own = expert_of == e
        wo[e] = tn(jnp.where(own, hid[...].astype(F32), 0.0).astype(BF16), sgr[...]).astype(BF16)
        store(wo.at[e], wo_h.at[e])
        wi[e] = tn(jnp.where(own, sin[...].astype(F32), 0.0).astype(BF16), pgr[...]).astype(BF16)
        store(wi.at[e], wi_h.at[e])
    for t in range(tg.shape[0] // CHUNK):
        k = pl.ds(t * CHUNK, CHUNK)
        tg[k, :] = tn(lhs[:, k], rhs[...]).astype(BF16)
        store(tg.at[k], tg_h.at[k])
    for cp in copies:
        cp.wait()


def on_device(tokens, slot_embed, w_in, w_out, cotangent):
    T, D = tokens.shape
    S = slot_embed.shape[0]
    E, _, F = w_in.shape
    V = pltpu.VMEM
    shape = jax.ShapeDtypeStruct
    blk = (48, 128)
    scratch = [
        V((T, D), BF16), V((S, D), BF16), V(w_in.shape, BF16), V(w_out.shape, BF16), V((T, D), BF16),
        V((S, T), F32), V((S, T), BF16), V((S, T), F32), V((S, T), BF16), V((S, 128), F32), V((S, 128), F32),
        V((128, D), F32), V((128, D + 128), BF16), V((128, D + 128), BF16),
        V((128, D + 128), BF16), V((3, 32, D + 128), BF16), V((8,) + blk, BF16), V((16,) + blk, BF16), V((4,) + blk, BF16),
        V((128, D), F32), V((128, D), BF16), V((128, D), BF16), V((4, 320, 128), BF16), V((3, 320, 128), BF16),
        V((8,) + blk, BF16), V((16,) + blk, BF16), V((4,) + blk, BF16),
        V((4,) + blk, BF16), V((16,) + blk, BF16), V((16, 4) + blk, BF16),
        V((4,) + blk, BF16), V((16,) + blk, BF16), V((8, 8) + blk, BF16),
        V((S, 128), F32), V((S, 128), F32),
        V((S, D // 2), F32), V((S, D // 2), BF16), V((S, D // 2), BF16), V((S, D // 2), BF16),
        V((16, 16, D // 2), BF16), V((2, 8, D // 2), F32), V((8, 8, D // 2), F32),
        pltpu.SemaphoreType.DMA((8,)),
        pltpu.SemaphoreType.DMA((N_GROUPS,)),
        pltpu.SemaphoreType.DMA((N_GROUPS,)),
    ]
    eg, lhs, rhs, slot_in, slot_grad, hidden, pre_grad = pl.pallas_call(
        main_kernel,
        name="moe_exchange",
        out_shape=[
            V((2, D), F32), V((2 * S, T), BF16), V((2 * S, D), BF16),
            V((16, D), BF16), V((16, D), BF16), V((16, F), BF16), V((16, F), BF16),
        ],
        in_specs=[pl.BlockSpec(memory_space=pltpu.HBM)] * 5,
        out_specs=[pl.BlockSpec(memory_space=pltpu.VMEM)] * 7,
        scratch_shapes=scratch,
        compiler_params=pltpu.CompilerParams(
            collective_id=0, has_side_effects=True, vmem_limit_bytes=52 * 2**20
        ),
    )(tokens, slot_embed, w_in, w_out, cotangent)
    embed_grad, token_grad, w_in_grad, w_out_grad = pl.pallas_call(
        grads_kernel,
        name="grads",
        out_shape=[shape((2, D), F32), shape((T, D), BF16), shape(w_in.shape, BF16), shape(w_out.shape, BF16)],
        in_specs=[pl.BlockSpec(memory_space=pltpu.VMEM)] * 7,
        out_specs=[pl.BlockSpec(memory_space=pl.ANY)] * 4,
        scratch_shapes=[
            V((T, D), BF16), V(w_in.shape, BF16), V(w_out.shape, BF16), pltpu.SemaphoreType.DMA((1 + 2 * E + T // CHUNK,)),
        ],
        compiler_params=pltpu.CompilerParams(vmem_limit_bytes=40 * 2**20),
    )(eg, lhs, rhs, slot_in, slot_grad, hidden, pre_grad)
    return (token_grad, embed_grad, w_in_grad, w_out_grad)


def solution(mesh):
    in_specs = (
        P(("seq", "expert"), None),
        P(),
        P("expert", None, "seq"),
        P("expert", "seq", None),
        P(("seq", "expert"), None),
    )
    out_specs = (
        P(("seq", "expert"), None),
        P(("seq", "expert"), None),
        P("expert", None, "seq"),
        P("expert", "seq", None),
    )
    return jax.shard_map(
        on_device, mesh=mesh, in_specs=in_specs, out_specs=out_specs, check_vma=False
    )
```

```python
import functools

import jax
import jax.numpy as jnp
from jax import lax
from jax.experimental import pallas as pl
from jax.experimental.pallas import tpu as pltpu
from jax.sharding import PartitionSpec as P

MESH = pl.DeviceIdType.MESH
F32 = jnp.float32
BF16 = jnp.bfloat16
CHUNK = 256
GELU_C = 0.7978845608028654
GELU_A = 0.044715


def coords():
    s = lax.axis_index("seq")
    e = lax.axis_index("expert")
    return s // 2, (s % 2) * 2 + e // 8, (e // 2) % 4, e % 2


def device(z, y, x, c):
    return (z * 2 + y // 2, (y % 2) * 8 + x * 2 + c)


def nn(a, b):
    return lax.dot_general(a, b, (((1,), (0,)), ((), ())), preferred_element_type=F32)


def nt(a, b):
    return lax.dot_general(a, b, (((1,), (1,)), ((), ())), preferred_element_type=F32)


def tn(a, b):
    return lax.dot_general(a, b, (((0,), (0,)), ((), ())), preferred_element_type=F32)


def hops(k):
    return min(k, 4 - k)


PLANE = sorted(
    ((a, b) for a in range(4) for b in range(4) if a or b), key=lambda p: -hops(p[0]) - hops(p[1])
)
RING = (2, 1, 3)


def rows_at(start, size, unit):
    return pl.ds(pl.multiple_of(start, unit), size)


def split3(v):
    hi = v.astype(BF16).astype(F32)
    mid = (v - hi).astype(BF16).astype(F32)
    lo = (v - hi - mid).astype(BF16).astype(F32)
    return hi, mid, lo


def scalar_tile(columns):
    parts = [p for v in columns for p in split3(v)]
    rows = columns[0].shape[0]
    lane = lax.broadcasted_iota(jnp.int32, (rows, 128), 1)
    tile = jnp.zeros((rows, 128), F32)
    for i, p in enumerate(parts):
        tile = jnp.where((lane >= 16 * i) & (lane < 16 * i + 16), p, tile)
    return tile


def scalar_of(tile, i):
    a = 48 * i
    return tile[:, a : a + 1] + tile[:, a + 16 : a + 17] + tile[:, a + 32 : a + 33]


def chunk_tiles(v16, z):
    h, q = z // 2, z % 2
    return [v16[8 * h : 8 * h + 8, 640 * q + 128 * j : 640 * q + 128 * j + 128] for j in range(5)]


def unpack_rows(blocks):
    out = []
    for j in range(10):
        q, jj = j // 5, j % 5
        out.append(
            jnp.concatenate([blocks[q][8 * jj : 8 * jj + 8], blocks[2 + q][8 * jj : 8 * jj + 8]], axis=0)
        )
    return out


class Group:
    def __init__(self, net, index, total):
        self.net, self.index, self.total = net, index, total

    def copy(self, src, dst, dev):
        return pltpu.make_async_remote_copy(
            src_ref=src, dst_ref=dst, send_sem=self.net.ss.at[self.index], recv_sem=self.net.rs.at[self.index],
            device_id=dev, device_id_type=MESH,
        )

    def put(self, src, dst, dev):
        self.copy(src, dst, dev).start()

    def wait_recv(self):
        self.copy(self.total, self.total, self.net.other).wait_recv()

    def wait_send(self):
        self.copy(self.total, self.total, self.net.other).wait_send()


class Net:
    def __init__(self, ss, rs, other):
        self.ss, self.rs, self.other, self.groups = ss, rs, other, []

    def group(self, total):
        g = Group(self, len(self.groups), total)
        self.groups.append(g)
        return g

    def put(self, src, dst, dev):
        g = self.group(dst)
        g.put(src, dst, dev)
        return g


N_GROUPS = 29
TILE0 = (8, 128)


def main_kernel(
    tok_h, emb_h, win_h, wout_h, cot_h,
    eg_o, lhs_o, rhs_o, wi_o, wo_o,
    tok, emb, win, wout, cot,
    lt, et, cf, cb, m_s, s_s,
    u_own, u_cs, u_cr, u_xs, u_xr, u_pk, u_yr, sall,
    g_own, g_cs, g_cr, g_pk, g_zr, g_pk2, g_yr, gall,
    o_pk, o_sr, oall, i_pk, i_sr, iall,
    l_all, inner_all,
    c_own, c_cs, c_cr, c_ys, c_yr, c_xs, c_xr,
    ld, ss, rs,
):
    z, y, x, c = coords()
    ylo, yhi = y % 2, y // 2
    oc = 1 - c
    D = tok.shape[1]
    other = device(z, y, x, oc)
    net = Net(ss, rs, other)

    loads = {}

    def load(name, src, dst):
        cp = pltpu.make_async_copy(src, dst, ld.at[len(loads)])
        cp.start()
        loads[name] = cp

    for cc in range(2):
        for xx in range(4):
            for yy in range(2):
                g = yy * 8 + xx * 2 + cc
                p = cc * 128 + xx * 32 + yy * 16
                pltpu.make_async_copy(emb_h.at[pl.ds(16 * g, 16)], emb.at[pl.ds(p, 16)], ld.at[0]).start()
    loads["emb"] = pltpu.make_async_copy(emb_h, emb, ld.at[0])
    n_chunks = tok.shape[0] // CHUNK
    for t in range(n_chunks):
        load(("tok", t), tok_h.at[pl.ds(t * CHUNK, CHUNK)], tok.at[pl.ds(t * CHUNK, CHUNK)])
    load("cot", cot_h, cot)
    load("win", win_h, win)
    load("wout", wout_h, wout)

    barrier = pltpu.get_barrier_semaphore()
    partners = [(z, y, x, oc)]
    partners += [((z + a) % 4, (y + b) % 4, x, c) for a in range(4) for b in range(4) if a or b]
    partners += [(z, (y + b) % 4, (x + a) % 4, c) for a in range(1, 4) for b in range(4)]
    partners += [(z, y, (x + a) % 4, oc) for a in range(1, 4)]
    partners += [((z + a) % 4, y, (x + b) % 4, c) for a in range(1, 4) for b in range(1, 4)]
    for p in partners:
        pl.semaphore_signal(barrier, inc=1, device_id=device(*p), device_id_type=MESH)

    loads["emb"].wait()
    for t in range(n_chunks):
        loads[("tok", t)].wait()
        lt[:, t * CHUNK : (t + 1) * CHUNK] = nt(emb[...], tok[t * CHUNK : (t + 1) * CHUNK, :])

    @pl.loop(0, 8, unroll=4)
    def _(i):
        r = rows_at(i * 32, 32, 32)
        l = lt[r, :]
        m = jnp.max(l, axis=1, keepdims=True)
        e = jnp.exp(l - m)
        s = jnp.sum(e, axis=1, keepdims=True)
        et[r, :] = e.astype(BF16)
        m_s[r, :] = jnp.broadcast_to(m, (32, 128))
        s_s[r, :] = jnp.broadcast_to(s, (32, 128))

    ro = rows_at(oc * 128, 128, 128)
    rc = rows_at(c * 128, 128, 128)
    w_o = et[ro, :]
    for n in range(D // 256):
        u_cs[:, n * 256 : (n + 1) * 256] = nn(w_o, tok[:, n * 256 : (n + 1) * 256]).astype(BF16)
    u_cs[:, D : D + 128] = scalar_tile([m_s[ro, 0:1], s_s[ro, 0:1]]).astype(BF16)
    pl.semaphore_wait(barrier, len(partners))
    u_core = net.put(u_cs, u_cr, device(z, y, x, oc))
    w_c = et[rc, :]
    for n in range(D // 256):
        u_own[:, n * 256 : (n + 1) * 256] = nn(w_c, tok[:, n * 256 : (n + 1) * 256])

    @pl.loop(0, n_chunks)
    def _(t):
        k = rows_at(t * CHUNK, CHUNK, CHUNK)
        l = lt[:, k]
        e = jnp.exp(l - jnp.max(l, axis=0, keepdims=True))
        f = e / jnp.sum(e, axis=0, keepdims=True)
        cf[:, k] = f
        cb[:, k] = f.astype(BF16)

    u_core.wait_recv()

    def merge_core(first):
        r = rows_at(first, 16, 16)
        rg = rows_at(c * 128 + first, 16, 16)
        v = u_cr[r, :].astype(F32)
        m1, s1 = m_s[rg, 0:1], s_s[rg, 0:1]
        sc = v[:, D : D + 128]
        m2, s2 = scalar_of(sc, 0), scalar_of(sc, 1)
        m = jnp.maximum(m1, m2)
        f1, f2 = jnp.exp(m1 - m), jnp.exp(m2 - m)
        s = s1 * f1 + s2 * f2
        u = u_own[r, :] * f1 + v[:, :D] * f2
        u_own[r, :] = u
        u_xs[r, :] = jnp.concatenate([u, scalar_tile([m, s])], axis=1).astype(BF16)
        m_s[rg, :] = jnp.broadcast_to(m, (16, 128))
        s_s[rg, :] = jnp.broadcast_to(s, (16, 128))

    u_x = net.group(u_xr)
    for k in RING + (0,):
        xx = (x + k) % 4
        merge_core(xx * 32)
        merge_core(xx * 32 + 16)
        if k:
            u_x.put(u_xs.at[rows_at(xx * 32, 32, 32)], u_xr.at[k - 1], device(z, y, xx, c))

    cot_load = loads["cot"]
    cot_load.wait()
    w_o = cb[ro, :]
    for n in range(D // 256):
        g_cs[:, n * 256 : (n + 1) * 256] = nn(w_o, cot[:, n * 256 : (n + 1) * 256]).astype(BF16)
    g_core = net.put(g_cs, g_cr, device(z, y, x, oc))
    w_c = cb[rc, :]
    for n in range(D // 256):
        g_own[:, n * 256 : (n + 1) * 256] = nn(w_c, cot[:, n * 256 : (n + 1) * 256])
    g_core.wait_recv()

    @pl.loop(0, 4, unroll=2)
    def _(i):
        r = rows_at(i * 32, 32, 32)
        v = g_own[r, :] + g_cr[r, :].astype(F32)
        for zz in range(4):
            tiles = chunk_tiles(v[:16], zz) + chunk_tiles(v[16:], zz)
            g_pk[zz, rows_at(i * 80, 80, 16), :] = jnp.concatenate(tiles, axis=0).astype(BF16)

    g_z = net.group(g_zr)
    for k in RING:
        zz = (z + k) % 4
        g_z.put(g_pk.at[zz], g_zr.at[k - 1], device(zz, y, x, c))

    u_x.wait_recv()
    for yy in range(2):
        r0 = x * 32 + yy * 16
        r = rows_at(r0, 16, 16)
        rg = rows_at(c * 128 + r0, 16, 16)
        ms, sums, us = [m_s[rg, 0:1]], [s_s[rg, 0:1]], [u_own[r, :]]
        for k in range(3):
            v = u_xr[k, yy * 16 : yy * 16 + 16, :].astype(F32)
            sc = v[:, D : D + 128]
            ms.append(scalar_of(sc, 0))
            sums.append(scalar_of(sc, 1))
            us.append(v[:, :D])
        m = functools.reduce(jnp.maximum, ms)
        fs = [jnp.exp(mk - m) for mk in ms]
        s = sum(a * f for a, f in zip(sums, fs))
        u = sum(a * f for a, f in zip(us, fs))
        for zz in range(4):
            h = zz // 2
            tile = scalar_tile([m[8 * h : 8 * h + 8], s[8 * h : 8 * h + 8]])
            u_pk[yy * 4 + zz] = jnp.concatenate(chunk_tiles(u, zz) + [tile], axis=0).astype(BF16)
    u_yz = net.group(u_yr.at[pl.ds(1, 15)])
    for a, b in PLANE:
        zz, yy = (z + a) % 4, (y + b) % 4
        u_yz.put(u_pk.at[(yy % 2) * 4 + zz], u_yr.at[a * 4 + b], device(zz, yy, x, c))
    u_yr[0] = u_pk[ylo * 4 + z]

    g_z.wait_recv()

    @pl.loop(0, 4, unroll=2)
    def _(i):
        r = rows_at(i * 80, 80, 16)
        v = g_pk[z, r, :].astype(F32)
        for k in range(3):
            v = v + g_zr[k, r, :].astype(F32)
        pad = jnp.zeros(TILE0, F32)
        g_pk2[2 * i] = jnp.concatenate([v[:40], pad], axis=0).astype(BF16)
        g_pk2[2 * i + 1] = jnp.concatenate([v[40:], pad], axis=0).astype(BF16)

    g_xy = net.group(g_yr.at[pl.ds(1, 15)])
    for a, b in PLANE:
        xx, yy = (x + a) % 4, (y + b) % 4
        g_xy.put(g_pk2.at[xx * 2 + yy % 2], g_yr.at[a * 4 + b], device(z, yy, xx, c))
    g_yr[0] = g_pk2[x * 2 + ylo]

    u_yz.wait_recv()
    parts = [u_yr[k].astype(F32) for k in range(16)]
    ms = [scalar_of(v[40:48], 0) for v in parts]
    sums = [scalar_of(v[40:48], 1) for v in parts]
    m = functools.reduce(jnp.maximum, ms)
    fs = [jnp.exp(mk - m) for mk in ms]
    s = sum(a * f for a, f in zip(sums, fs))
    lse = m + jnp.log(s)
    lse_tile = scalar_tile([lse])
    tiles = []
    for j in range(5):
        tiles.append(sum(v[8 * j : 8 * j + 8] * f for v, f in zip(parts, fs)) / s)
    sall[z] = jnp.concatenate(tiles + [lse_tile], axis=0).astype(BF16)
    u_ag = net.group(sall.at[pl.ds(0, 3)])
    for k in RING:
        u_ag.put(sall.at[z], sall.at[z], device((z + k) % 4, y, x, c))

    g_xy.wait_recv()
    acc = g_yr[0].astype(F32)
    for k in range(1, 16):
        acc = acc + g_yr[k].astype(F32)
    gall[z] = acc.astype(BF16)
    g_ag = net.group(gall.at[pl.ds(0, 3)])
    for k in RING:
        g_ag.put(gall.at[z], gall.at[z], device((z + k) % 4, y, x, c))
    loads["win"].wait()
    loads["wout"].wait()
    u_ag.wait_recv()

    F = win.shape[2]
    expert_of = lax.broadcasted_iota(jnp.int32, (16, 1), 0) // 4
    slot_in_f = jnp.concatenate(unpack_rows([sall[k].astype(F32) for k in range(4)]), axis=1)
    slot_in = slot_in_f.astype(BF16)
    pre = jnp.zeros((16, F), F32)
    for e in range(4):
        pre = jnp.where(expert_of == e, nn(slot_in, win[e]), pre)
    th = jnp.tanh(GELU_C * (pre + GELU_A * pre * pre * pre))
    hidden_f = 0.5 * pre * (1.0 + th)
    slope = 0.5 * (1.0 + th) + 0.5 * pre * (1.0 - th * th) * GELU_C * (1.0 + 3.0 * GELU_A * pre * pre)
    out_part = jnp.zeros((16, D), F32)
    for e in range(4):
        out_part += nn(jnp.where(expert_of == e, hidden_f, 0.0).astype(BF16), wout[e])
    for zz in range(4):
        tile = sall[zz, 40:48, :].astype(F32)
        o_pk[zz] = jnp.concatenate(chunk_tiles(out_part, zz) + [tile], axis=0).astype(BF16)

    def seq_sums(pk, sr):
        group = net.group(sr.at[pl.ds(1, 15)])
        for a, b in PLANE:
            zz = (z + a) % 4
            group.put(pk.at[zz], sr.at[a * 4 + b], device(zz, (y + b) % 4, x, c))
        sr[0] = pk[z]
        return group

    def seq_total(sr, parity, rows):
        ks = [a * 4 + b for a in range(4) for b in range(4) if b % 2 == parity]
        acc = sr[ks[0], 0:rows, :].astype(F32)
        for k in ks[1:]:
            acc = acc + sr[k, 0:rows, :].astype(F32)
        return acc

    o_seq = seq_sums(o_pk, o_sr)

    g_ag.wait_recv()

    slot_grad = jnp.concatenate(unpack_rows([gall[k].astype(F32) for k in range(4)]), axis=1).astype(BF16)
    hid_grad = jnp.zeros((16, F), F32)
    for e in range(4):
        hid_grad = jnp.where(expert_of == e, nt(slot_grad, wout[e]), hid_grad)
    pre_grad = (hid_grad * slope).astype(BF16)
    in_part = jnp.zeros((16, D), F32)
    for e in range(4):
        in_part = jnp.where(expert_of == e, nt(pre_grad, win[e]), in_part)
    inner_part = jnp.sum(pre * pre_grad.astype(F32), axis=1, keepdims=True)
    for zz in range(4):
        h = zz // 2
        tile = scalar_tile([inner_part[8 * h : 8 * h + 8]])
        i_pk[zz] = jnp.concatenate(chunk_tiles(in_part, zz) + [tile], axis=0).astype(BF16)
    i_seq = seq_sums(i_pk, i_sr)

    for e in range(4):
        own = expert_of == e
        wo_o[e] = tn(jnp.where(own, hidden_f, 0.0).astype(BF16), slot_grad).astype(BF16)
        wi_o[e] = tn(jnp.where(own, slot_in_f, 0.0).astype(BF16), pre_grad).astype(BF16)

    o_seq.wait_recv()
    pair = c * 8 + x * 2
    for parity in range(2):
        acc = seq_total(o_sr, parity, 40)
        lse_tile = o_sr[parity, 40:48, :].astype(F32)
        oall[pair + (ylo + parity) % 2, z] = jnp.concatenate([acc, lse_tile], axis=0).astype(BF16)
    o_all = [net.group(oall.at[pl.ds(0, 2), pl.ds(0, 3)])] + [net.group(oall.at[pl.ds(0, 2)]) for _ in range(3)]
    ref = oall.at[pl.ds(pair, 2), z]
    for k, a in PLANE:
        o_all[k].put(ref, ref, device((z + a) % 4, y, (x + k) % 4, c))

    i_seq.wait_recv()
    cz = c * 4 + z
    for parity in range(2):
        acc = seq_total(i_sr, parity, 48)
        inner = scalar_of(acc[40:48], 0)
        block = jnp.concatenate([acc[:40], scalar_tile([inner])], axis=0)
        iall[cz, x * 2 + (ylo + parity) % 2] = block.astype(BF16)
    i_all = [net.group(iall.at[0, pl.ds(0, 6)])] + [net.group(iall.at[0]) for _ in range(3)]
    ref = iall.at[cz, pl.ds(x * 2, 2)]
    for k, a in PLANE:
        i_all[k].put(ref, ref, device((z + k) % 4, y, (x + a) % 4, c))

    half = rhs_o.shape[0] // 2

    def place(i, blocks, scalars):
        r = rows_at(i * 16, 16, 16)
        for j, t in enumerate(unpack_rows(blocks)):
            rhs_o[r, j * 128 : (j + 1) * 128] = t.astype(BF16)
        v = jnp.concatenate([scalar_of(blocks[0][40:48], 0), scalar_of(blocks[2][40:48], 0)], axis=0)
        scalars[r, :] = jnp.broadcast_to(v, (16, 128))

    def place_out(first):
        for i in range(2):
            place(first + i, [oall[first + i, k].astype(F32) for k in range(4)], l_all)

    def place_in(core):
        @pl.loop(0, 8, unroll=4)
        def _(k):
            place(core * 8 + k, [iall[core * 4 + zz, k].astype(F32) for zz in range(4)], inner_all)

    o_3, i_3 = [], []
    for k in range(4):
        o_all[k].wait_recv()
        first = c * 8 + ((x - k + 4) % 4) * 2
        ref = oall.at[pl.ds(first, 2)]
        o_3.append(net.put(ref, ref, other))
        place_out(first)
    for k in range(4):
        o_3[k].wait_recv()
        place_out(oc * 8 + ((x - k + 4) % 4) * 2)
    for k in range(4):
        i_all[k].wait_recv()
        ref = iall.at[c * 4 + (z - k + 4) % 4]
        i_3.append(net.put(ref, ref, other))

    @pl.loop(0, n_chunks, unroll=2)
    def _(t):
        k = rows_at(t * CHUNK, CHUNK, CHUNK)
        cg = nt(rhs_o[0:half, :], cot[k, :])
        f = cf[:, k]
        cf[:, k] = f * (cg - jnp.sum(f * cg, axis=0, keepdims=True))
        df = jnp.exp(lt[:, k] - l_all[:, 0:1])
        lt[:, k] = df
        lhs_o[0:half, k] = df.astype(BF16)

    place_in(c)
    for cp in i_3:
        cp.wait_recv()
    place_in(oc)
    rhs_o[half:, :] = emb[...]

    @pl.loop(0, n_chunks, unroll=2)
    def _(t):
        k = rows_at(t * CHUNK, CHUNK, CHUNK)
        dg = nt(rhs_o[0:half, :], tok[k, :])
        lhs_o[half:, k] = (lt[:, k] * (dg - inner_all[:, 0:1]) + cf[:, k]).astype(BF16)

    H = D // 2
    pieces = ((0, 384), (384, 256))
    c_core = net.group(c_cr)
    for a, b in pieces:
        c_cs[:, a : a + b] = nn(lhs_o[half:, :], tok[:, rows_at(oc * H + a, b, 128)]).astype(BF16)
        c_core.put(c_cs.at[:, a : a + b], c_cr.at[:, a : a + b], other)
    for a, b in pieces:
        c_own[:, a : a + b] = nn(lhs_o[half:, :], tok[:, rows_at(c * H + a, b, 128)])
    c_core.wait_recv()

    @pl.loop(0, 16, unroll=4)
    def _(i):
        r = rows_at(i * 16, 16, 16)
        c_ys[r, :] = (c_own[r, :] + c_cr[r, :].astype(F32)).astype(BF16)

    def block_of(zz, yy):
        return rows_at((yy % 2) * 128 + ((zz % 2) * 2 + yy // 2) * 32 + (zz // 2) * 16, 16, 16)

    c_y = net.group(c_yr.at[pl.ds(1, 15)])
    for a, b in PLANE:
        zz, yy = (z + a) % 4, (y + b) % 4
        c_y.put(c_ys.at[block_of(zz, yy)], c_yr.at[a * 4 + b], device(zz, yy, x, c))
    c_yr[0] = c_ys[block_of(z, y), :]
    c_y.wait_recv()
    acc = c_yr[0].astype(F32)
    for k in range(1, 16):
        acc = acc + c_yr[k].astype(F32)
    blocks = H // 128
    at = lax.broadcasted_iota(jnp.int32, (128, 16 * blocks), 0)
    of = lax.broadcasted_iota(jnp.int32, (128, 16 * blocks), 1)
    t_of, r_of = of // 16, of % 16
    pick = at == (r_of // 2) * 16 + 2 * t_of + r_of % 2
    stacked = jnp.concatenate([acc[:, 128 * t : 128 * t + 128] for t in range(blocks)], axis=0).astype(BF16)
    packed = nn(jnp.where(pick, 1.0, 0.0).astype(BF16), stacked)
    for j in range(8):
        c_xs[j] = packed[16 * j : 16 * j + 16].astype(BF16)
    c_x = net.group(c_xr.at[pl.ds(1, 7)])
    for k in RING + (0,):
        for d in range(2):
            if k or d:
                xx, cc = (x + k) % 4, c if d == 0 else oc
                c_x.put(c_xs.at[xx * 2 + cc], c_xr.at[k * 2 + d], device(z, y, xx, cc))
    c_xr[0] = c_xs[x * 2 + c]
    c_x.wait_recv()
    for d in range(2):
        v = sum(c_xr[2 * k + d].astype(F32) for k in range(4))
        out = jnp.concatenate([v[2 * t : 2 * t + 2] for t in range(blocks)], axis=1)
        eg_o[:, rows_at((c if d == 0 else oc) * H, H, 128)] = out

    for g in net.groups:
        g.wait_send()


def grads_kernel(eg, lhs, rhs, wi, wo, eg_h, tg_h, wi_h, wo_h, tg, sem):
    copies = []

    def store(src, dst):
        cp = pltpu.make_async_copy(src, dst, sem.at[len(copies)])
        cp.start()
        copies.append(cp)

    store(wi, wi_h)
    store(wo, wo_h)
    store(eg, eg_h)
    T = tg.shape[0]
    for t in range(T // CHUNK):
        k = pl.ds(t * CHUNK, CHUNK)
        tg[k, :] = tn(lhs[:, k], rhs[...]).astype(BF16)
        if t % 2:
            k = pl.ds((t - 1) * CHUNK, 2 * CHUNK)
            store(tg.at[k], tg_h.at[k])
    for cp in copies:
        cp.wait()


def on_device(tokens, slot_embed, w_in, w_out, cotangent):
    T, D = tokens.shape
    S = slot_embed.shape[0]
    E, _, F = w_in.shape
    V = pltpu.VMEM
    shape = jax.ShapeDtypeStruct
    blk = (48, 128)
    scratch = [
        V((T, D), BF16), V((S, D), BF16), V(w_in.shape, BF16), V(w_out.shape, BF16), V((T, D), BF16),
        V((S, T), F32), V((S, T), BF16), V((S, T), F32), V((S, T), BF16), V((S, 128), F32), V((S, 128), F32),
        V((128, D), F32), V((128, D + 128), BF16), V((128, D + 128), BF16),
        V((128, D + 128), BF16), V((3, 32, D + 128), BF16), V((8,) + blk, BF16), V((16,) + blk, BF16), V((4,) + blk, BF16),
        V((128, D), F32), V((128, D), BF16), V((128, D), BF16), V((4, 320, 128), BF16), V((3, 320, 128), BF16),
        V((8,) + blk, BF16), V((16,) + blk, BF16), V((4,) + blk, BF16),
        V((4,) + blk, BF16), V((16,) + blk, BF16), V((16, 4) + blk, BF16),
        V((4,) + blk, BF16), V((16,) + blk, BF16), V((8, 8) + blk, BF16),
        V((S, 128), F32), V((S, 128), F32),
        V((S, D // 2), F32), V((S, D // 2), BF16), V((S, D // 2), BF16), V((S, D // 2), BF16),
        V((16, 16, D // 2), BF16), V((8, 16, 128), BF16), V((8, 16, 128), BF16),
        pltpu.SemaphoreType.DMA((8,)),
        pltpu.SemaphoreType.DMA((N_GROUPS,)),
        pltpu.SemaphoreType.DMA((N_GROUPS,)),
    ]
    eg, lhs, rhs, wi, wo = pl.pallas_call(
        main_kernel,
        name="moe_exchange",
        out_shape=[
            V((2, D), F32), V((2 * S, T), BF16), V((2 * S, D), BF16),
            V(w_in.shape, BF16), V(w_out.shape, BF16),
        ],
        in_specs=[pl.BlockSpec(memory_space=pltpu.HBM)] * 5,
        out_specs=[pl.BlockSpec(memory_space=pltpu.VMEM)] * 5,
        scratch_shapes=scratch,
        compiler_params=pltpu.CompilerParams(
            collective_id=0, has_side_effects=True, vmem_limit_bytes=52 * 2**20
        ),
    )(tokens, slot_embed, w_in, w_out, cotangent)
    embed_grad, token_grad, w_in_grad, w_out_grad = pl.pallas_call(
        grads_kernel,
        name="grads",
        out_shape=[shape((2, D), F32), shape((T, D), BF16), shape(w_in.shape, BF16), shape(w_out.shape, BF16)],
        in_specs=[pl.BlockSpec(memory_space=pltpu.VMEM)] * 5,
        out_specs=[pl.BlockSpec(memory_space=pl.ANY)] * 4,
        scratch_shapes=[
            V((T, D), BF16), pltpu.SemaphoreType.DMA((3 + T // (2 * CHUNK),)),
        ],
        compiler_params=pltpu.CompilerParams(vmem_limit_bytes=40 * 2**20),
    )(eg, lhs, rhs, wi, wo)
    return (token_grad, embed_grad, w_in_grad, w_out_grad)


def solution(mesh):
    in_specs = (
        P(("seq", "expert"), None),
        P(),
        P("expert", None, "seq"),
        P("expert", "seq", None),
        P(("seq", "expert"), None),
    )
    out_specs = (
        P(("seq", "expert"), None),
        P(("seq", "expert"), None),
        P("expert", None, "seq"),
        P("expert", "seq", None),
    )
    return jax.shard_map(
        on_device, mesh=mesh, in_specs=in_specs, out_specs=out_specs, check_vma=False
    )
```

```python
import functools

import jax
import jax.numpy as jnp
from jax import lax
from jax.experimental import pallas as pl
from jax.experimental.pallas import tpu as pltpu
from jax.sharding import PartitionSpec as P

MESH = pl.DeviceIdType.MESH
F32 = jnp.float32
BF16 = jnp.bfloat16
CHUNK = 256
GELU_C = 0.7978845608028654
GELU_A = 0.044715


def coords():
    s = lax.axis_index("seq")
    e = lax.axis_index("expert")
    return s // 2, (s % 2) * 2 + e // 8, (e // 2) % 4, e % 2


def device(z, y, x, c):
    return (z * 2 + y // 2, (y % 2) * 8 + x * 2 + c)


def nn(a, b):
    return lax.dot_general(a, b, (((1,), (0,)), ((), ())), preferred_element_type=F32)


def nt(a, b):
    return lax.dot_general(a, b, (((1,), (1,)), ((), ())), preferred_element_type=F32)


def tn(a, b):
    return lax.dot_general(a, b, (((0,), (0,)), ((), ())), preferred_element_type=F32)


def hops(k):
    return min(k, 4 - k)


PLANE = sorted(
    ((a, b) for a in range(4) for b in range(4) if a or b), key=lambda p: -hops(p[0]) - hops(p[1])
)
RING = (2, 1, 3)


def rows_at(start, size, unit):
    return pl.ds(pl.multiple_of(start, unit), size)


def split3(v):
    hi = v.astype(BF16).astype(F32)
    mid = (v - hi).astype(BF16).astype(F32)
    lo = (v - hi - mid).astype(BF16).astype(F32)
    return hi, mid, lo


def scalar_tile(columns):
    parts = [p for v in columns for p in split3(v)]
    rows = columns[0].shape[0]
    lane = lax.broadcasted_iota(jnp.int32, (rows, 128), 1)
    tile = jnp.zeros((rows, 128), F32)
    for i, p in enumerate(parts):
        tile = jnp.where((lane >= 16 * i) & (lane < 16 * i + 16), p, tile)
    return tile


def scalar_of(tile, i):
    a = 48 * i
    return tile[:, a : a + 1] + tile[:, a + 16 : a + 17] + tile[:, a + 32 : a + 33]


def chunk_tiles(v16, z):
    h, q = z // 2, z % 2
    return [v16[8 * h : 8 * h + 8, 640 * q + 128 * j : 640 * q + 128 * j + 128] for j in range(5)]


def unpack_rows(blocks):
    out = []
    for j in range(10):
        q, jj = j // 5, j % 5
        out.append(
            jnp.concatenate([blocks[q][8 * jj : 8 * jj + 8], blocks[2 + q][8 * jj : 8 * jj + 8]], axis=0)
        )
    return out


class Group:
    def __init__(self, net, index, total):
        self.net, self.index, self.total = net, index, total

    def copy(self, src, dst, dev):
        return pltpu.make_async_remote_copy(
            src_ref=src, dst_ref=dst, send_sem=self.net.ss.at[self.index], recv_sem=self.net.rs.at[self.index],
            device_id=dev, device_id_type=MESH,
        )

    def put(self, src, dst, dev):
        self.copy(src, dst, dev).start()

    def wait_recv(self):
        self.copy(self.total, self.total, self.net.other).wait_recv()

    def wait_send(self):
        self.copy(self.total, self.total, self.net.other).wait_send()


class Net:
    def __init__(self, ss, rs, other):
        self.ss, self.rs, self.other, self.groups = ss, rs, other, []

    def group(self, total):
        g = Group(self, len(self.groups), total)
        self.groups.append(g)
        return g

    def put(self, src, dst, dev):
        g = self.group(dst)
        g.put(src, dst, dev)
        return g


N_GROUPS = 29
TILE0 = (8, 128)


def main_kernel(
    tok_h, emb_h, win_h, wout_h, cot_h,
    eg_o, tg_o, wi_o, wo_o,
    lhs, rhs, win_t, wout_t, tok_t, cot_t,
    tok, emb5, win, wout, cot,
    lt, et, cf, cb, m_s, s_s,
    u_own, u_cs, u_cr, u_xs, u_xr, u_pk, u_yr, sall,
    g_own, g_cs, g_cr, g_pk, g_zr, g_pk2, g_yr, gall,
    o_pk, o_sr, oall, i_pk, i_sr, iall,
    l_all, inner_all,
    c_own, c_cs, c_cr, c_ys, c_yr, c_xs, c_xr,
    ld, ss, rs,
):
    z, y, x, c = coords()
    ylo, yhi = y % 2, y // 2
    oc = 1 - c
    D = tok.shape[1]
    other = device(z, y, x, oc)
    net = Net(ss, rs, other)

    loads = {}

    def load(name, src, dst):
        cp = pltpu.make_async_copy(src, dst, ld.at[len(loads)])
        cp.start()
        loads[name] = cp

    for cc in range(2):
        for yy in range(2):
            pltpu.make_async_copy(emb_h.at[yy, :, cc], emb5.at[cc, :, yy], ld.at[0]).start()
    loads["emb"] = pltpu.make_async_copy(emb_h, emb5, ld.at[0])
    n_chunks = tok.shape[0] // CHUNK
    for t in range(n_chunks):
        load(("tok", t), tok_h.at[pl.ds(t * CHUNK, CHUNK)], tok.at[pl.ds(t * CHUNK, CHUNK)])
    load("cot", cot_h, cot)
    load("win", win_h, win)
    load("wout", wout_h, wout)

    barrier = pltpu.get_barrier_semaphore()
    partners = [(z, y, x, oc)]
    partners += [((z + a) % 4, (y + b) % 4, x, c) for a in range(4) for b in range(4) if a or b]
    partners += [(z, (y + b) % 4, (x + a) % 4, c) for a in range(1, 4) for b in range(4)]
    partners += [(z, y, (x + a) % 4, oc) for a in range(1, 4)]
    partners += [((z + a) % 4, y, (x + b) % 4, c) for a in range(1, 4) for b in range(1, 4)]
    for p in partners:
        pl.semaphore_signal(barrier, inc=1, device_id=device(*p), device_id_type=MESH)

    loads["emb"].wait()
    emb = emb5[...].reshape(-1, D)
    for t in range(n_chunks):
        loads[("tok", t)].wait()
        lt[:, t * CHUNK : (t + 1) * CHUNK] = nt(emb, tok[t * CHUNK : (t + 1) * CHUNK, :])

    @pl.loop(0, 8, unroll=4)
    def _(i):
        r = rows_at(i * 32, 32, 32)
        l = lt[r, :]
        m = jnp.max(l, axis=1, keepdims=True)
        e = jnp.exp(l - m)
        s = jnp.sum(e, axis=1, keepdims=True)
        et[r, :] = e.astype(BF16)
        m_s[r, :] = jnp.broadcast_to(m, (32, 128))
        s_s[r, :] = jnp.broadcast_to(s, (32, 128))

    ro = rows_at(oc * 128, 128, 128)
    rc = rows_at(c * 128, 128, 128)
    w_o = et[ro, :]
    for n in range(D // 256):
        u_cs[:, n * 256 : (n + 1) * 256] = nn(w_o, tok[:, n * 256 : (n + 1) * 256]).astype(BF16)
    u_cs[:, D : D + 128] = scalar_tile([m_s[ro, 0:1], s_s[ro, 0:1]]).astype(BF16)
    pl.semaphore_wait(barrier, len(partners))
    u_core = net.put(u_cs, u_cr, device(z, y, x, oc))
    w_c = et[rc, :]
    for n in range(D // 256):
        u_own[:, n * 256 : (n + 1) * 256] = nn(w_c, tok[:, n * 256 : (n + 1) * 256])

    @pl.loop(0, n_chunks)
    def _(t):
        k = rows_at(t * CHUNK, CHUNK, CHUNK)
        l = lt[:, k]
        e = jnp.exp(l - jnp.max(l, axis=0, keepdims=True))
        f = e / jnp.sum(e, axis=0, keepdims=True)
        cf[:, k] = f
        cb[:, k] = f.astype(BF16)

    u_core.wait_recv()

    def merge_core(first):
        r = rows_at(first, 16, 16)
        rg = rows_at(c * 128 + first, 16, 16)
        v = u_cr[r, :].astype(F32)
        m1, s1 = m_s[rg, 0:1], s_s[rg, 0:1]
        sc = v[:, D : D + 128]
        m2, s2 = scalar_of(sc, 0), scalar_of(sc, 1)
        m = jnp.maximum(m1, m2)
        f1, f2 = jnp.exp(m1 - m), jnp.exp(m2 - m)
        s = s1 * f1 + s2 * f2
        u = u_own[r, :] * f1 + v[:, :D] * f2
        u_own[r, :] = u
        u_xs[r, :] = jnp.concatenate([u, scalar_tile([m, s])], axis=1).astype(BF16)
        m_s[rg, :] = jnp.broadcast_to(m, (16, 128))
        s_s[rg, :] = jnp.broadcast_to(s, (16, 128))

    u_x = net.group(u_xr)
    for k in RING + (0,):
        xx = (x + k) % 4
        merge_core(xx * 32)
        merge_core(xx * 32 + 16)
        if k:
            u_x.put(u_xs.at[rows_at(xx * 32, 32, 32)], u_xr.at[k - 1], device(z, y, xx, c))

    cot_load = loads["cot"]
    cot_load.wait()
    w_o = cb[ro, :]
    for n in range(D // 256):
        g_cs[:, n * 256 : (n + 1) * 256] = nn(w_o, cot[:, n * 256 : (n + 1) * 256]).astype(BF16)
    g_core = net.put(g_cs, g_cr, device(z, y, x, oc))
    w_c = cb[rc, :]
    for n in range(D // 256):
        g_own[:, n * 256 : (n + 1) * 256] = nn(w_c, cot[:, n * 256 : (n + 1) * 256])
    g_core.wait_recv()

    @pl.loop(0, 4, unroll=2)
    def _(i):
        r = rows_at(i * 32, 32, 32)
        v = g_own[r, :] + g_cr[r, :].astype(F32)
        for zz in range(4):
            tiles = chunk_tiles(v[:16], zz) + chunk_tiles(v[16:], zz)
            g_pk[zz, rows_at(i * 80, 80, 16), :] = jnp.concatenate(tiles, axis=0).astype(BF16)

    g_z = net.group(g_zr)
    for k in RING:
        zz = (z + k) % 4
        g_z.put(g_pk.at[zz], g_zr.at[k - 1], device(zz, y, x, c))

    loads["win"].wait()
    loads["wout"].wait()
    for e in range(4):
        wout_t[e] = wout[e].T
        win_t[e] = win[e].T

    u_x.wait_recv()
    for yy in range(2):
        r0 = x * 32 + yy * 16
        r = rows_at(r0, 16, 16)
        rg = rows_at(c * 128 + r0, 16, 16)
        ms, sums, us = [m_s[rg, 0:1]], [s_s[rg, 0:1]], [u_own[r, :]]
        for k in range(3):
            v = u_xr[k, yy * 16 : yy * 16 + 16, :].astype(F32)
            sc = v[:, D : D + 128]
            ms.append(scalar_of(sc, 0))
            sums.append(scalar_of(sc, 1))
            us.append(v[:, :D])
        m = functools.reduce(jnp.maximum, ms)
        fs = [jnp.exp(mk - m) for mk in ms]
        s = sum(a * f for a, f in zip(sums, fs))
        u = sum(a * f for a, f in zip(us, fs))
        for zz in range(4):
            h = zz // 2
            tile = scalar_tile([m[8 * h : 8 * h + 8], s[8 * h : 8 * h + 8]])
            u_pk[yy * 4 + zz] = jnp.concatenate(chunk_tiles(u, zz) + [tile], axis=0).astype(BF16)
    u_yz = net.group(u_yr.at[pl.ds(1, 15)])
    for a, b in PLANE:
        zz, yy = (z + a) % 4, (y + b) % 4
        u_yz.put(u_pk.at[(yy % 2) * 4 + zz], u_yr.at[a * 4 + b], device(zz, yy, x, c))
    u_yr[0] = u_pk[ylo * 4 + z]

    g_z.wait_recv()

    @pl.loop(0, 4, unroll=2)
    def _(i):
        r = rows_at(i * 80, 80, 16)
        v = g_pk[z, r, :].astype(F32)
        for k in range(3):
            v = v + g_zr[k, r, :].astype(F32)
        pad = jnp.zeros(TILE0, F32)
        g_pk2[2 * i] = jnp.concatenate([v[:40], pad], axis=0).astype(BF16)
        g_pk2[2 * i + 1] = jnp.concatenate([v[40:], pad], axis=0).astype(BF16)

    g_xy = net.group(g_yr.at[pl.ds(1, 15)])
    for a, b in PLANE:
        xx, yy = (x + a) % 4, (y + b) % 4
        g_xy.put(g_pk2.at[xx * 2 + yy % 2], g_yr.at[a * 4 + b], device(z, yy, xx, c))
    g_yr[0] = g_pk2[x * 2 + ylo]

    for t in range(n_chunks):
        k = pl.ds(t * CHUNK, CHUNK)
        tok_t[:, k] = tok[k, :].T
        cot_t[:, k] = cot[k, :].T

    u_yz.wait_recv()
    parts = [u_yr[k].astype(F32) for k in range(16)]
    ms = [scalar_of(v[40:48], 0) for v in parts]
    sums = [scalar_of(v[40:48], 1) for v in parts]
    m = functools.reduce(jnp.maximum, ms)
    fs = [jnp.exp(mk - m) for mk in ms]
    s = sum(a * f for a, f in zip(sums, fs))
    lse = m + jnp.log(s)
    lse_tile = scalar_tile([lse])
    tiles = []
    for j in range(5):
        tiles.append(sum(v[8 * j : 8 * j + 8] * f for v, f in zip(parts, fs)) / s)
    sall[z] = jnp.concatenate(tiles + [lse_tile], axis=0).astype(BF16)
    u_ag = net.group(sall.at[pl.ds(0, 3)])
    for k in RING:
        u_ag.put(sall.at[z], sall.at[z], device((z + k) % 4, y, x, c))

    g_xy.wait_recv()
    acc = g_yr[0].astype(F32)
    for k in range(1, 16):
        acc = acc + g_yr[k].astype(F32)
    gall[z] = acc.astype(BF16)
    g_ag = net.group(gall.at[pl.ds(0, 3)])
    for k in RING:
        g_ag.put(gall.at[z], gall.at[z], device((z + k) % 4, y, x, c))
    u_ag.wait_recv()

    F = win.shape[2]
    expert_of = lax.broadcasted_iota(jnp.int32, (16, 1), 0) // 4
    slot_in_f = jnp.concatenate(unpack_rows([sall[k].astype(F32) for k in range(4)]), axis=1)
    slot_in = slot_in_f.astype(BF16)
    pre = jnp.zeros((16, F), F32)
    for e in range(4):
        pre = jnp.where(expert_of == e, nn(slot_in, win[e]), pre)
    th = jnp.tanh(GELU_C * (pre + GELU_A * pre * pre * pre))
    hidden_f = 0.5 * pre * (1.0 + th)
    slope = 0.5 * (1.0 + th) + 0.5 * pre * (1.0 - th * th) * GELU_C * (1.0 + 3.0 * GELU_A * pre * pre)
    out_part = jnp.zeros((16, D), F32)
    for e in range(4):
        out_part += nn(jnp.where(expert_of == e, hidden_f, 0.0).astype(BF16), wout[e])
    for zz in range(4):
        tile = sall[zz, 40:48, :].astype(F32)
        o_pk[zz] = jnp.concatenate(chunk_tiles(out_part, zz) + [tile], axis=0).astype(BF16)

    def seq_sums(pk, sr, by_z):
        group = net.group(sr.at[pl.ds(1, 15)])
        for a, b in PLANE:
            zz, yy = (z + a) % 4, (y + b) % 4
            group.put(pk.at[zz if by_z else yy], sr.at[a * 4 + b], device(zz, yy, x, c))
        sr[0] = pk[z if by_z else y]
        return group

    def seq_total(sr, parity, rows):
        ks = [a * 4 + b for a in range(4) for b in range(4) if b % 2 == parity]
        acc = sr[ks[0], 0:rows, :].astype(F32)
        for k in ks[1:]:
            acc = acc + sr[k, 0:rows, :].astype(F32)
        return acc

    o_seq = seq_sums(o_pk, o_sr, True)

    g_ag.wait_recv()

    slot_grad = jnp.concatenate(unpack_rows([gall[k].astype(F32) for k in range(4)]), axis=1).astype(BF16)
    hid_grad = jnp.zeros((16, F), F32)
    for e in range(4):
        hid_grad = jnp.where(expert_of == e, nn(slot_grad, wout_t[e]), hid_grad)
    pre_grad = (hid_grad * slope).astype(BF16)
    in_part = jnp.zeros((16, D), F32)
    for e in range(4):
        in_part = jnp.where(expert_of == e, nn(pre_grad, win_t[e]), in_part)
    inner_part = jnp.sum(pre * pre_grad.astype(F32), axis=1, keepdims=True)
    for zz in range(4):
        h = zz // 2
        tile = scalar_tile([inner_part[8 * h : 8 * h + 8]])
        i_pk[zz] = jnp.concatenate(chunk_tiles(in_part, zz) + [tile], axis=0).astype(BF16)
    i_seq = seq_sums(i_pk, i_sr, False)

    for e in range(4):
        own = expert_of == e
        wo_o[e] = tn(jnp.where(own, hidden_f, 0.0).astype(BF16), slot_grad).astype(BF16)
        wi_o[e] = tn(jnp.where(own, slot_in_f, 0.0).astype(BF16), pre_grad).astype(BF16)

    o_seq.wait_recv()
    pair = c * 8 + x * 2
    for parity in range(2):
        acc = seq_total(o_sr, parity, 40)
        lse_tile = o_sr[parity, 40:48, :].astype(F32)
        oall[pair + (ylo + parity) % 2, z] = jnp.concatenate([acc, lse_tile], axis=0).astype(BF16)
    o_all = [net.group(oall.at[pl.ds(0, 2), pl.ds(0, 3)])] + [net.group(oall.at[pl.ds(0, 2)]) for _ in range(3)]
    ref = oall.at[pl.ds(pair, 2), z]
    for k, a in PLANE:
        o_all[k].put(ref, ref, device((z + a) % 4, y, (x + k) % 4, c))

    i_seq.wait_recv()
    cy = c * 4 + y
    for parity in range(2):
        acc = seq_total(i_sr, parity, 48)
        inner = scalar_of(acc[40:48], 0)
        block = jnp.concatenate([acc[:40], scalar_tile([inner])], axis=0)
        iall[cy, x * 2 + (ylo + parity) % 2] = block.astype(BF16)
    i_all = [net.group(iall.at[0, pl.ds(0, 6)])] + [net.group(iall.at[0]) for _ in range(3)]
    ref = iall.at[cy, pl.ds(x * 2, 2)]
    for k, a in PLANE:
        i_all[k].put(ref, ref, device(z, (y + k) % 4, (x + a) % 4, c))

    half = rhs.shape[0] // 2

    def place(i, blocks, scalars):
        r = rows_at(i * 16, 16, 16)
        for j, t in enumerate(unpack_rows(blocks)):
            rhs[r, j * 128 : (j + 1) * 128] = t.astype(BF16)
        v = jnp.concatenate([scalar_of(blocks[0][40:48], 0), scalar_of(blocks[2][40:48], 0)], axis=0)
        scalars[r, :] = jnp.broadcast_to(v, (16, 128))

    def place_out(first):
        for i in range(2):
            place(first + i, [oall[first + i, k].astype(F32) for k in range(4)], l_all)

    def place_in(core):
        @pl.loop(0, 8, unroll=4)
        def _(k):
            place(core * 8 + k, [iall[core * 4 + zz, k].astype(F32) for zz in range(4)], inner_all)

    o_3, i_3 = [], []
    for k in range(4):
        o_all[k].wait_recv()
        first = c * 8 + ((x - k + 4) % 4) * 2
        ref = oall.at[pl.ds(first, 2)]
        o_3.append(net.put(ref, ref, other))
        place_out(first)
    for k in range(4):
        o_3[k].wait_recv()
        place_out(oc * 8 + ((x - k + 4) % 4) * 2)
    for k in range(4):
        i_all[k].wait_recv()
        ref = iall.at[c * 4 + (y - k + 4) % 4]
        i_3.append(net.put(ref, ref, other))

    @pl.loop(0, n_chunks, unroll=2)
    def _(t):
        k = rows_at(t * CHUNK, CHUNK, CHUNK)
        cg = nn(rhs[0:half, :], cot_t[:, k])
        f = cf[:, k]
        cf[:, k] = f * (cg - jnp.sum(f * cg, axis=0, keepdims=True))
        df = jnp.exp(lt[:, k] - l_all[:, 0:1])
        lt[:, k] = df
        lhs[0:half, k] = df.astype(BF16)

    H = D // 2
    pieces = ((0, 384), (384, 256))
    c_core = net.group(c_cr)

    def tail(core):
        place_in(core)
        rows = rows_at(core * 128, 128, 128)
        rows_g = rows_at(half + core * 128, 128, 128)
        for t in range(n_chunks):
            k = pl.ds(t * CHUNK, CHUNK)
            dg = nn(rhs[rows, :], tok_t[:, k])
            lhs[rows_g, k] = (lt[rows, k] * (dg - inner_all[rows, 0:1]) + cf[rows, k]).astype(BF16)
        w = lhs[rows_g, :]
        for a, b in pieces:
            c_cs[rows, a : a + b] = nn(w, tok[:, rows_at(oc * H + a, b, 128)]).astype(BF16)
        c_core.put(c_cs.at[rows], c_cr.at[rows], other)
        for a, b in pieces:
            c_own[rows, a : a + b] = nn(w, tok[:, rows_at(c * H + a, b, 128)])

    tail(c)
    for cp in i_3:
        cp.wait_recv()
    tail(oc)
    c_core.wait_recv()

    @pl.loop(0, 16, unroll=4)
    def _(i):
        r = rows_at(i * 16, 16, 16)
        c_ys[r, :] = (c_own[r, :] + c_cr[r, :].astype(F32)).astype(BF16)

    def block_of(zz, yy):
        return rows_at((yy % 2) * 128 + ((zz % 2) * 2 + yy // 2) * 32 + (zz // 2) * 16, 16, 16)

    c_y = net.group(c_yr.at[pl.ds(1, 15)])
    for a, b in PLANE:
        zz, yy = (z + a) % 4, (y + b) % 4
        c_y.put(c_ys.at[block_of(zz, yy)], c_yr.at[a * 4 + b], device(zz, yy, x, c))
    c_yr[0] = c_ys[block_of(z, y), :]
    rhs[half:, :] = emb5[...].reshape(-1, D)
    for t in range(n_chunks):
        k = pl.ds(t * CHUNK, CHUNK)
        tg_o[k, :] = tn(lhs[:, k], rhs[...]).astype(BF16)
    c_y.wait_recv()
    acc = c_yr[0].astype(F32)
    for k in range(1, 16):
        acc = acc + c_yr[k].astype(F32)
    blocks = H // 128
    at = lax.broadcasted_iota(jnp.int32, (128, 16 * blocks), 0)
    of = lax.broadcasted_iota(jnp.int32, (128, 16 * blocks), 1)
    t_of, r_of = of // 16, of % 16
    pick = at == (r_of // 2) * 16 + 2 * t_of + r_of % 2
    stacked = jnp.concatenate([acc[:, 128 * t : 128 * t + 128] for t in range(blocks)], axis=0).astype(BF16)
    packed = nn(jnp.where(pick, 1.0, 0.0).astype(BF16), stacked)
    for j in range(8):
        c_xs[j] = packed[16 * j : 16 * j + 16].astype(BF16)
    c_x = net.group(c_xr.at[pl.ds(1, 7)])
    for k in RING + (0,):
        for d in range(2):
            if k or d:
                xx, cc = (x + k) % 4, c if d == 0 else oc
                c_x.put(c_xs.at[xx * 2 + cc], c_xr.at[k * 2 + d], device(z, y, xx, cc))
    c_xr[0] = c_xs[x * 2 + c]
    c_x.wait_recv()
    for d in range(2):
        v = sum(c_xr[2 * k + d].astype(F32) for k in range(4))
        out = jnp.concatenate([v[2 * t : 2 * t + 2] for t in range(blocks)], axis=1)
        eg_o[:, rows_at((c if d == 0 else oc) * H, H, 128)] = out

    for g in net.groups:
        g.wait_send()


def write_kernel(eg, tg, wi, wo, eg_h, tg_h, wi_h, wo_h, sem):
    copies = [
        pltpu.make_async_copy(src, dst, sem.at[i])
        for i, (src, dst) in enumerate(((eg, eg_h), (wi, wi_h), (wo, wo_h), (tg, tg_h)))
    ]
    for cp in copies:
        cp.start()
    for cp in copies:
        cp.wait()


def on_device(tokens, slot_embed, w_in, w_out, cotangent):
    T, D = tokens.shape
    S = slot_embed.shape[0]
    E, _, F = w_in.shape
    V = pltpu.VMEM
    shape = jax.ShapeDtypeStruct
    blk = (48, 128)
    scratch = [
        V((2 * S, T), BF16), V((2 * S, D), BF16),
        V((E, F, D), BF16), V((E, D, F), BF16), V((D, T), BF16), V((D, T), BF16),
        V((T, D), BF16), V((2, 4, 2, 16, D), BF16), V(w_in.shape, BF16), V(w_out.shape, BF16), V((T, D), BF16),
        V((S, T), F32), V((S, T), BF16), V((S, T), F32), V((S, T), BF16), V((S, 128), F32), V((S, 128), F32),
        V((128, D), F32), V((128, D + 128), BF16), V((128, D + 128), BF16),
        V((128, D + 128), BF16), V((3, 32, D + 128), BF16), V((8,) + blk, BF16), V((16,) + blk, BF16), V((4,) + blk, BF16),
        V((128, D), F32), V((128, D), BF16), V((128, D), BF16), V((4, 320, 128), BF16), V((3, 320, 128), BF16),
        V((8,) + blk, BF16), V((16,) + blk, BF16), V((4,) + blk, BF16),
        V((4,) + blk, BF16), V((16,) + blk, BF16), V((16, 4) + blk, BF16),
        V((4,) + blk, BF16), V((16,) + blk, BF16), V((8, 8) + blk, BF16),
        V((S, 128), F32), V((S, 128), F32),
        V((S, D // 2), F32), V((S, D // 2), BF16), V((S, D // 2), BF16), V((S, D // 2), BF16),
        V((16, 16, D // 2), BF16), V((8, 16, 128), BF16), V((8, 16, 128), BF16),
        pltpu.SemaphoreType.DMA((8,)),
        pltpu.SemaphoreType.DMA((N_GROUPS,)),
        pltpu.SemaphoreType.DMA((N_GROUPS,)),
    ]
    outs = pl.pallas_call(
        main_kernel,
        name="moe_exchange",
        out_shape=[
            V((2, D), F32), V((T, D), BF16), V(w_in.shape, BF16), V(w_out.shape, BF16),
        ],
        in_specs=[pl.BlockSpec(memory_space=pltpu.HBM)] * 5,
        out_specs=[pl.BlockSpec(memory_space=pltpu.VMEM)] * 4,
        scratch_shapes=scratch,
        compiler_params=pltpu.CompilerParams(
            collective_id=0, has_side_effects=True, vmem_limit_bytes=52 * 2**20
        ),
    )(tokens, slot_embed.reshape(2, 4, 2, 16, D), w_in, w_out, cotangent)
    embed_grad, token_grad, w_in_grad, w_out_grad = pl.pallas_call(
        write_kernel,
        name="write",
        out_shape=[shape((2, D), F32), shape((T, D), BF16), shape(w_in.shape, BF16), shape(w_out.shape, BF16)],
        in_specs=[pl.BlockSpec(memory_space=pltpu.VMEM)] * 4,
        out_specs=[pl.BlockSpec(memory_space=pl.ANY)] * 4,
        scratch_shapes=[pltpu.SemaphoreType.DMA((4,))],
        compiler_params=pltpu.CompilerParams(vmem_limit_bytes=40 * 2**20),
    )(*outs)
    return (token_grad, embed_grad, w_in_grad, w_out_grad)


def solution(mesh):
    in_specs = (
        P(("seq", "expert"), None),
        P(),
        P("expert", None, "seq"),
        P("expert", "seq", None),
        P(("seq", "expert"), None),
    )
    out_specs = (
        P(("seq", "expert"), None),
        P(("seq", "expert"), None),
        P("expert", None, "seq"),
        P("expert", "seq", None),
    )
    return jax.shard_map(
        on_device, mesh=mesh, in_specs=in_specs, out_specs=out_specs, check_vma=False
    )
```

```python
import functools

import jax
import jax.numpy as jnp
from jax import lax
from jax.experimental import pallas as pl
from jax.experimental.pallas import tpu as pltpu
from jax.sharding import PartitionSpec as P

MESH = pl.DeviceIdType.MESH
F32 = jnp.float32
BF16 = jnp.bfloat16
CHUNK = 256
GELU_C = 0.7978845608028654
GELU_A = 0.044715


def coords():
    s = lax.axis_index("seq")
    e = lax.axis_index("expert")
    return s // 2, (s % 2) * 2 + e // 8, (e // 2) % 4, e % 2


def device(z, y, x, c):
    return (z * 2 + y // 2, (y % 2) * 8 + x * 2 + c)


def nn(a, b):
    return lax.dot_general(a, b, (((1,), (0,)), ((), ())), preferred_element_type=F32)


def nt(a, b):
    return lax.dot_general(a, b, (((1,), (1,)), ((), ())), preferred_element_type=F32)


def tn(a, b):
    return lax.dot_general(a, b, (((0,), (0,)), ((), ())), preferred_element_type=F32)


def hops(k):
    return min(k, 4 - k)


PLANE = sorted(
    ((a, b) for a in range(4) for b in range(4) if a or b), key=lambda p: -hops(p[0]) - hops(p[1])
)
RING = (2, 1, 3)


def rows_at(start, size, unit):
    return pl.ds(pl.multiple_of(start, unit), size)


def split3(v):
    hi = v.astype(BF16).astype(F32)
    mid = (v - hi).astype(BF16).astype(F32)
    lo = (v - hi - mid).astype(BF16).astype(F32)
    return hi, mid, lo


def scalar_tile(columns):
    parts = [p for v in columns for p in split3(v)]
    rows = columns[0].shape[0]
    lane = lax.broadcasted_iota(jnp.int32, (rows, 128), 1)
    tile = jnp.zeros((rows, 128), F32)
    for i, p in enumerate(parts):
        tile = jnp.where((lane >= 16 * i) & (lane < 16 * i + 16), p, tile)
    return tile


def scalar_of(tile, i):
    a = 48 * i
    return tile[:, a : a + 1] + tile[:, a + 16 : a + 17] + tile[:, a + 32 : a + 33]


def chunk_tiles(v16, z):
    h, q = z // 2, z % 2
    return [v16[8 * h : 8 * h + 8, 640 * q + 128 * j : 640 * q + 128 * j + 128] for j in range(5)]


def unpack_rows(blocks):
    out = []
    for j in range(10):
        q, jj = j // 5, j % 5
        out.append(
            jnp.concatenate([blocks[q][8 * jj : 8 * jj + 8], blocks[2 + q][8 * jj : 8 * jj + 8]], axis=0)
        )
    return out


class Group:
    def __init__(self, net, index, total):
        self.net, self.index, self.total = net, index, total

    def copy(self, src, dst, dev):
        return pltpu.make_async_remote_copy(
            src_ref=src, dst_ref=dst, send_sem=self.net.ss.at[self.index], recv_sem=self.net.rs.at[self.index],
            device_id=dev, device_id_type=MESH,
        )

    def put(self, src, dst, dev):
        self.copy(src, dst, dev).start()

    def wait_recv(self):
        self.copy(self.total, self.total, self.net.other).wait_recv()

    def wait_send(self):
        self.copy(self.total, self.total, self.net.other).wait_send()


class Net:
    def __init__(self, ss, rs, other):
        self.ss, self.rs, self.other, self.groups = ss, rs, other, []

    def group(self, total):
        g = Group(self, len(self.groups), total)
        self.groups.append(g)
        return g

    def put(self, src, dst, dev):
        g = self.group(dst)
        g.put(src, dst, dev)
        return g


N_GROUPS = 29
TILE0 = (8, 128)


def main_kernel(
    tok_h, emb_h, win_h, wout_h, cot_h,
    eg_o, tg_o, wi_o, wo_o,
    lhs, rhs, win_t, wout_t, tok_t, cot_t,
    tok, emb5, win, wout, cot,
    lt, et, cf, cb, m_s, s_s,
    u_own, u_cs, u_cr, u_xs, u_xr, u_pk, u_yr, sall,
    g_own, g_cs, g_cr, g_pk, g_zr, g_pk2, g_yr, gall,
    o_pk, o_sr, oall, i_pk, i_sr, iall,
    l_all, inner_all,
    c_own, c_cs, c_cr, c_ys, c_yr, c_xs, c_xr,
    ld, ss, rs,
):
    z, y, x, c = coords()
    ylo, yhi = y % 2, y // 2
    oc = 1 - c
    D = tok.shape[1]
    other = device(z, y, x, oc)
    net = Net(ss, rs, other)

    loads = {}

    def load(name, src, dst):
        cp = pltpu.make_async_copy(src, dst, ld.at[len(loads)])
        cp.start()
        loads[name] = cp

    for cc in range(2):
        for yy in range(2):
            pltpu.make_async_copy(emb_h.at[yy, :, cc], emb5.at[cc, :, yy], ld.at[0]).start()
    loads["emb"] = pltpu.make_async_copy(emb_h, emb5, ld.at[0])
    n_chunks = tok.shape[0] // CHUNK
    for t in range(n_chunks):
        load(("tok", t), tok_h.at[pl.ds(t * CHUNK, CHUNK)], tok.at[pl.ds(t * CHUNK, CHUNK)])
    load("cot", cot_h, cot)
    load("win", win_h, win)
    load("wout", wout_h, wout)

    barrier = pltpu.get_barrier_semaphore()
    partners = [(z, y, x, oc)]
    partners += [((z + a) % 4, (y + b) % 4, x, c) for a in range(4) for b in range(4) if a or b]
    partners += [(z, (y + b) % 4, (x + a) % 4, c) for a in range(1, 4) for b in range(4)]
    partners += [(z, y, (x + a) % 4, oc) for a in range(1, 4)]
    partners += [((z + a) % 4, y, (x + b) % 4, c) for a in range(1, 4) for b in range(1, 4)]
    for p in partners:
        pl.semaphore_signal(barrier, inc=1, device_id=device(*p), device_id_type=MESH)

    loads["emb"].wait()
    emb = emb5[...].reshape(-1, D)
    for t in range(n_chunks):
        loads[("tok", t)].wait()
        lt[:, t * CHUNK : (t + 1) * CHUNK] = nt(emb, tok[t * CHUNK : (t + 1) * CHUNK, :])

    ro = rows_at(oc * 128, 128, 128)
    rc = rows_at(c * 128, 128, 128)

    @pl.loop(0, n_chunks, unroll=2)
    def _(t):
        k = rows_at(t * CHUNK, CHUNK, CHUNK)
        l = lt[:, k]
        e = jnp.exp(l - jnp.max(l, axis=0, keepdims=True))
        f = e / jnp.sum(e, axis=0, keepdims=True)
        cf[:, k] = f
        cb[:, k] = f.astype(BF16)

    cot_load = loads["cot"]
    cot_load.wait()
    w_o = cb[ro, :]
    for n in range(D // 256):
        g_cs[:, n * 256 : (n + 1) * 256] = nn(w_o, cot[:, n * 256 : (n + 1) * 256]).astype(BF16)
    pl.semaphore_wait(barrier, len(partners))
    g_core = net.put(g_cs, g_cr, device(z, y, x, oc))

    @pl.loop(0, 8, unroll=4)
    def _(i):
        r = rows_at(i * 32, 32, 32)
        l = lt[r, :]
        m = jnp.max(l, axis=1, keepdims=True)
        e = jnp.exp(l - m)
        s = jnp.sum(e, axis=1, keepdims=True)
        et[r, :] = e.astype(BF16)
        m_s[r, :] = jnp.broadcast_to(m, (32, 128))
        s_s[r, :] = jnp.broadcast_to(s, (32, 128))

    w_o = et[ro, :]
    for n in range(D // 256):
        u_cs[:, n * 256 : (n + 1) * 256] = nn(w_o, tok[:, n * 256 : (n + 1) * 256]).astype(BF16)
    u_cs[:, D : D + 128] = scalar_tile([m_s[ro, 0:1], s_s[ro, 0:1]]).astype(BF16)
    u_core = net.put(u_cs, u_cr, device(z, y, x, oc))
    w_c = cb[rc, :]
    for n in range(D // 256):
        g_own[:, n * 256 : (n + 1) * 256] = nn(w_c, cot[:, n * 256 : (n + 1) * 256])
    g_core.wait_recv()

    @pl.loop(0, 4, unroll=2)
    def _(i):
        r = rows_at(i * 32, 32, 32)
        v = g_own[r, :] + g_cr[r, :].astype(F32)
        for zz in range(4):
            tiles = chunk_tiles(v[:16], zz) + chunk_tiles(v[16:], zz)
            g_pk[zz, rows_at(i * 80, 80, 16), :] = jnp.concatenate(tiles, axis=0).astype(BF16)

    g_z = net.group(g_zr)
    for k in RING:
        zz = (z + k) % 4
        g_z.put(g_pk.at[zz], g_zr.at[k - 1], device(zz, y, x, c))

    w_c = et[rc, :]
    for n in range(D // 256):
        u_own[:, n * 256 : (n + 1) * 256] = nn(w_c, tok[:, n * 256 : (n + 1) * 256])

    u_core.wait_recv()

    def merge_core(first):
        r = rows_at(first, 16, 16)
        rg = rows_at(c * 128 + first, 16, 16)
        v = u_cr[r, :].astype(F32)
        m1, s1 = m_s[rg, 0:1], s_s[rg, 0:1]
        sc = v[:, D : D + 128]
        m2, s2 = scalar_of(sc, 0), scalar_of(sc, 1)
        m = jnp.maximum(m1, m2)
        f1, f2 = jnp.exp(m1 - m), jnp.exp(m2 - m)
        s = s1 * f1 + s2 * f2
        u = u_own[r, :] * f1 + v[:, :D] * f2
        u_own[r, :] = u
        u_xs[r, :] = jnp.concatenate([u, scalar_tile([m, s])], axis=1).astype(BF16)
        m_s[rg, :] = jnp.broadcast_to(m, (16, 128))
        s_s[rg, :] = jnp.broadcast_to(s, (16, 128))

    u_x = net.group(u_xr)
    for k in RING + (0,):
        xx = (x + k) % 4
        merge_core(xx * 32)
        merge_core(xx * 32 + 16)
        if k:
            u_x.put(u_xs.at[rows_at(xx * 32, 32, 32)], u_xr.at[k - 1], device(z, y, xx, c))

    loads["win"].wait()
    loads["wout"].wait()
    for e in range(4):
        wout_t[e] = wout[e].T
        win_t[e] = win[e].T

    g_z.wait_recv()

    @pl.loop(0, 4, unroll=2)
    def _(i):
        r = rows_at(i * 80, 80, 16)
        v = g_pk[z, r, :].astype(F32)
        for k in range(3):
            v = v + g_zr[k, r, :].astype(F32)
        pad = jnp.zeros(TILE0, F32)
        g_pk2[2 * i] = jnp.concatenate([v[:40], pad], axis=0).astype(BF16)
        g_pk2[2 * i + 1] = jnp.concatenate([v[40:], pad], axis=0).astype(BF16)

    g_xy = net.group(g_yr.at[pl.ds(1, 15)])
    for a, b in PLANE:
        xx, yy = (x + a) % 4, (y + b) % 4
        g_xy.put(g_pk2.at[xx * 2 + yy % 2], g_yr.at[a * 4 + b], device(z, yy, xx, c))
    g_yr[0] = g_pk2[x * 2 + ylo]

    u_x.wait_recv()
    for yy in range(2):
        r0 = x * 32 + yy * 16
        r = rows_at(r0, 16, 16)
        rg = rows_at(c * 128 + r0, 16, 16)
        ms, sums, us = [m_s[rg, 0:1]], [s_s[rg, 0:1]], [u_own[r, :]]
        for k in range(3):
            v = u_xr[k, yy * 16 : yy * 16 + 16, :].astype(F32)
            sc = v[:, D : D + 128]
            ms.append(scalar_of(sc, 0))
            sums.append(scalar_of(sc, 1))
            us.append(v[:, :D])
        m = functools.reduce(jnp.maximum, ms)
        fs = [jnp.exp(mk - m) for mk in ms]
        s = sum(a * f for a, f in zip(sums, fs))
        u = sum(a * f for a, f in zip(us, fs))
        tile = scalar_tile([m, s])
        for zz in range(4):
            h = zz // 2
            tiles = chunk_tiles(u, zz) + [tile[8 * h : 8 * h + 8]]
            u_pk[yy * 4 + zz] = jnp.concatenate(tiles, axis=0).astype(BF16)
    u_yz = net.group(u_yr.at[pl.ds(1, 15)])
    for a, b in PLANE:
        zz, yy = (z + a) % 4, (y + b) % 4
        u_yz.put(u_pk.at[(yy % 2) * 4 + zz], u_yr.at[a * 4 + b], device(zz, yy, x, c))
    u_yr[0] = u_pk[ylo * 4 + z]

    for t in range(n_chunks):
        k = pl.ds(t * CHUNK, CHUNK)
        tok_t[:, k] = tok[k, :].T
        cot_t[:, k] = cot[k, :].T

    g_xy.wait_recv()
    acc = g_yr[0].astype(F32)
    for k in range(1, 16):
        acc = acc + g_yr[k].astype(F32)
    gall[z] = acc.astype(BF16)
    g_ag = net.group(gall.at[pl.ds(0, 3)])
    for k in RING:
        g_ag.put(gall.at[z], gall.at[z], device((z + k) % 4, y, x, c))

    u_yz.wait_recv()
    parts = [u_yr[k].astype(F32) for k in range(16)]
    ms = [scalar_of(v[40:48], 0) for v in parts]
    sums = [scalar_of(v[40:48], 1) for v in parts]
    m = functools.reduce(jnp.maximum, ms)
    fs = [jnp.exp(mk - m) for mk in ms]
    s = sum(a * f for a, f in zip(sums, fs))
    lse = m + jnp.log(s)
    lse_tile = scalar_tile([lse])
    tiles = []
    for j in range(5):
        tiles.append(sum(v[8 * j : 8 * j + 8] * f for v, f in zip(parts, fs)) / s)
    sall[z] = jnp.concatenate(tiles + [lse_tile], axis=0).astype(BF16)
    u_ag = net.group(sall.at[pl.ds(0, 3)])
    for k in RING:
        u_ag.put(sall.at[z], sall.at[z], device((z + k) % 4, y, x, c))

    def seq_sums(pk, sr, by_z):
        group = net.group(sr.at[pl.ds(1, 15)])
        for a, b in PLANE:
            zz, yy = (z + a) % 4, (y + b) % 4
            group.put(pk.at[zz if by_z else yy], sr.at[a * 4 + b], device(zz, yy, x, c))
        sr[0] = pk[z if by_z else y]
        return group

    def seq_total(sr, parity, rows):
        ks = [a * 4 + b for a in range(4) for b in range(4) if b % 2 == parity]
        acc = sr[ks[0], 0:rows, :].astype(F32)
        for k in ks[1:]:
            acc = acc + sr[k, 0:rows, :].astype(F32)
        return acc

    F = win.shape[2]
    expert_of = lax.broadcasted_iota(jnp.int32, (16, 1), 0) // 4
    g_ag.wait_recv()
    slot_grad = jnp.concatenate(unpack_rows([gall[k].astype(F32) for k in range(4)]), axis=1).astype(BF16)
    hid_grad = jnp.zeros((16, F), F32)
    for e in range(4):
        hid_grad = jnp.where(expert_of == e, nn(slot_grad, wout_t[e]), hid_grad)
    u_ag.wait_recv()
    slot_in_f = jnp.concatenate(unpack_rows([sall[k].astype(F32) for k in range(4)]), axis=1)
    slot_in = slot_in_f.astype(BF16)
    pre = jnp.zeros((16, F), F32)
    hidden_f = jnp.zeros((16, F), F32)
    pre_grad = jnp.zeros((16, F), F32)
    out_part = jnp.zeros((16, D), F32)
    for e in range(4):
        own = expert_of == e
        v = nn(slot_in, win[e])
        th = jnp.tanh(GELU_C * (v + GELU_A * v * v * v))
        act = jnp.where(own, 0.5 * v * (1.0 + th), 0.0)
        slope = 0.5 * (1.0 + th) + 0.5 * v * (1.0 - th * th) * GELU_C * (1.0 + 3.0 * GELU_A * v * v)
        out_part += nn(act.astype(BF16), wout[e])
        hidden_f += act
        pre = jnp.where(own, v, pre)
        pre_grad += jnp.where(own, hid_grad * slope, 0.0)
    for zz in range(4):
        tile = sall[zz, 40:48, :].astype(F32)
        o_pk[zz] = jnp.concatenate(chunk_tiles(out_part, zz) + [tile], axis=0).astype(BF16)
    o_seq = seq_sums(o_pk, o_sr, True)
    in_part = jnp.zeros((16, D), F32)
    for e in range(4):
        in_part += nn(jnp.where(expert_of == e, pre_grad, 0.0).astype(BF16), win_t[e])
    pre_grad = pre_grad.astype(BF16)
    inner_part = jnp.sum(pre * pre_grad.astype(F32), axis=1, keepdims=True)
    tile = scalar_tile([inner_part])
    for zz in range(4):
        h = zz // 2
        tiles = chunk_tiles(in_part, zz) + [tile[8 * h : 8 * h + 8]]
        i_pk[zz] = jnp.concatenate(tiles, axis=0).astype(BF16)
    i_seq = seq_sums(i_pk, i_sr, False)

    for e in range(4):
        own = expert_of == e
        wo_o[e] = tn(jnp.where(own, hidden_f, 0.0).astype(BF16), slot_grad).astype(BF16)
        wi_o[e] = tn(jnp.where(own, slot_in_f, 0.0).astype(BF16), pre_grad).astype(BF16)

    o_seq.wait_recv()
    pair = c * 8 + x * 2
    for parity in range(2):
        acc = seq_total(o_sr, parity, 40)
        lse_tile = o_sr[parity, 40:48, :].astype(F32)
        oall[pair + (ylo + parity) % 2, z] = jnp.concatenate([acc, lse_tile], axis=0).astype(BF16)
    o_all = [net.group(oall.at[pl.ds(0, 2), pl.ds(0, 3)])] + [net.group(oall.at[pl.ds(0, 2)]) for _ in range(3)]
    ref = oall.at[pl.ds(pair, 2), z]
    for k, a in PLANE:
        o_all[k].put(ref, ref, device((z + a) % 4, y, (x + k) % 4, c))

    i_seq.wait_recv()
    cy = c * 4 + y
    for parity in range(2):
        acc = seq_total(i_sr, parity, 48)
        inner = scalar_of(acc[40:48], 0)
        block = jnp.concatenate([acc[:40], scalar_tile([inner])], axis=0)
        iall[cy, x * 2 + (ylo + parity) % 2] = block.astype(BF16)
    i_all = [net.group(iall.at[0, pl.ds(0, 6)])] + [net.group(iall.at[0]) for _ in range(3)]
    ref = iall.at[cy, pl.ds(x * 2, 2)]
    for k, a in PLANE:
        i_all[k].put(ref, ref, device(z, (y + k) % 4, (x + a) % 4, c))

    half = rhs.shape[0] // 2

    def place(i, blocks, scalars):
        r = rows_at(i * 16, 16, 16)
        for j, t in enumerate(unpack_rows(blocks)):
            rhs[r, j * 128 : (j + 1) * 128] = t.astype(BF16)
        v = jnp.concatenate([scalar_of(blocks[0][40:48], 0), scalar_of(blocks[2][40:48], 0)], axis=0)
        scalars[r, :] = jnp.broadcast_to(v, (16, 128))

    def place_out(first):
        for i in range(2):
            place(first + i, [oall[first + i, k].astype(F32) for k in range(4)], l_all)

    def place_in(core):
        @pl.loop(0, 8, unroll=8)
        def _(k):
            place(core * 8 + k, [iall[core * 4 + zz, k].astype(F32) for zz in range(4)], inner_all)

    o_3, i_3 = [], []
    for k in range(4):
        o_all[k].wait_recv()
        first = c * 8 + ((x - k + 4) % 4) * 2
        ref = oall.at[pl.ds(first, 2)]
        o_3.append(net.put(ref, ref, other))
        place_out(first)
    for k in range(4):
        o_3[k].wait_recv()
        place_out(oc * 8 + ((x - k + 4) % 4) * 2)
    for k in range(4):
        i_all[k].wait_recv()
        ref = iall.at[c * 4 + (y - k + 4) % 4]
        i_3.append(net.put(ref, ref, other))

    @pl.loop(0, n_chunks, unroll=2)
    def _(t):
        k = rows_at(t * CHUNK, CHUNK, CHUNK)
        cg = nn(rhs[0:half, :], cot_t[:, k])
        f = cf[:, k]
        cf[:, k] = f * (cg - jnp.sum(f * cg, axis=0, keepdims=True))
        df = jnp.exp(lt[:, k] - l_all[:, 0:1])
        lt[:, k] = df
        lhs[0:half, k] = df.astype(BF16)

    H = D // 2
    pieces = ((0, 384), (384, 256))
    c_core = net.group(c_cr)

    def tail(core):
        place_in(core)
        rows = rows_at(core * 128, 128, 128)
        rows_g = rows_at(half + core * 128, 128, 128)
        for t in range(n_chunks):
            k = pl.ds(t * CHUNK, CHUNK)
            dg = nn(rhs[rows, :], tok_t[:, k])
            lhs[rows_g, k] = (lt[rows, k] * (dg - inner_all[rows, 0:1]) + cf[rows, k]).astype(BF16)
        w = lhs[rows_g, :]
        for a, b in pieces:
            c_cs[rows, a : a + b] = nn(w, tok[:, rows_at(oc * H + a, b, 128)]).astype(BF16)
        c_core.put(c_cs.at[rows], c_cr.at[rows], other)
        for a, b in pieces:
            c_own[rows, a : a + b] = nn(w, tok[:, rows_at(c * H + a, b, 128)])

    tail(c)
    for cp in i_3:
        cp.wait_recv()
    tail(oc)
    c_core.wait_recv()

    @pl.loop(0, 16, unroll=4)
    def _(i):
        r = rows_at(i * 16, 16, 16)
        c_ys[r, :] = (c_own[r, :] + c_cr[r, :].astype(F32)).astype(BF16)

    def block_of(zz, yy):
        return rows_at((yy % 2) * 128 + ((zz % 2) * 2 + yy // 2) * 32 + (zz // 2) * 16, 16, 16)

    c_y = net.group(c_yr.at[pl.ds(1, 15)])
    for a, b in PLANE:
        zz, yy = (z + a) % 4, (y + b) % 4
        c_y.put(c_ys.at[block_of(zz, yy)], c_yr.at[a * 4 + b], device(zz, yy, x, c))
    c_yr[0] = c_ys[block_of(z, y), :]
    rhs[half:, :] = emb5[...].reshape(-1, D)
    for t in range(n_chunks):
        k = pl.ds(t * CHUNK, CHUNK)
        tg_o[k, :] = tn(lhs[:, k], rhs[...]).astype(BF16)
    c_y.wait_recv()
    acc = c_yr[0].astype(F32)
    for k in range(1, 16):
        acc = acc + c_yr[k].astype(F32)
    blocks = H // 128
    at = lax.broadcasted_iota(jnp.int32, (128, 16 * blocks), 0)
    of = lax.broadcasted_iota(jnp.int32, (128, 16 * blocks), 1)
    t_of, r_of = of // 16, of % 16
    pick = at == (r_of // 2) * 16 + 2 * t_of + r_of % 2
    stacked = jnp.concatenate([acc[:, 128 * t : 128 * t + 128] for t in range(blocks)], axis=0).astype(BF16)
    packed = nn(jnp.where(pick, 1.0, 0.0).astype(BF16), stacked)
    for j in range(8):
        c_xs[j] = packed[16 * j : 16 * j + 16].astype(BF16)
    c_x = net.group(c_xr.at[pl.ds(1, 7)])
    for k in RING + (0,):
        for d in range(2):
            if k or d:
                xx, cc = (x + k) % 4, c if d == 0 else oc
                c_x.put(c_xs.at[xx * 2 + cc], c_xr.at[k * 2 + d], device(z, y, xx, cc))
    c_xr[0] = c_xs[x * 2 + c]
    c_x.wait_recv()
    for d in range(2):
        v = sum(c_xr[2 * k + d].astype(F32) for k in range(4))
        out = jnp.concatenate([v[2 * t : 2 * t + 2] for t in range(blocks)], axis=1)
        eg_o[:, rows_at((c if d == 0 else oc) * H, H, 128)] = out

    for g in net.groups:
        g.wait_send()


def write_kernel(eg, tg, wi, wo, eg_h, tg_h, wi_h, wo_h, sem):
    copies = [
        pltpu.make_async_copy(src, dst, sem.at[i])
        for i, (src, dst) in enumerate(((eg, eg_h), (wi, wi_h), (wo, wo_h), (tg, tg_h)))
    ]
    for cp in copies:
        cp.start()
    for cp in copies:
        cp.wait()


def on_device(tokens, slot_embed, w_in, w_out, cotangent):
    T, D = tokens.shape
    S = slot_embed.shape[0]
    E, _, F = w_in.shape
    V = pltpu.VMEM
    shape = jax.ShapeDtypeStruct
    blk = (48, 128)
    scratch = [
        V((2 * S, T), BF16), V((2 * S, D), BF16),
        V((E, F, D), BF16), V((E, D, F), BF16), V((D, T), BF16), V((D, T), BF16),
        V((T, D), BF16), V((2, 4, 2, 16, D), BF16), V(w_in.shape, BF16), V(w_out.shape, BF16), V((T, D), BF16),
        V((S, T), F32), V((S, T), BF16), V((S, T), F32), V((S, T), BF16), V((S, 128), F32), V((S, 128), F32),
        V((128, D), F32), V((128, D + 128), BF16), V((128, D + 128), BF16),
        V((128, D + 128), BF16), V((3, 32, D + 128), BF16), V((8,) + blk, BF16), V((16,) + blk, BF16), V((4,) + blk, BF16),
        V((128, D), F32), V((128, D), BF16), V((128, D), BF16), V((4, 320, 128), BF16), V((3, 320, 128), BF16),
        V((8,) + blk, BF16), V((16,) + blk, BF16), V((4,) + blk, BF16),
        V((4,) + blk, BF16), V((16,) + blk, BF16), V((16, 4) + blk, BF16),
        V((4,) + blk, BF16), V((16,) + blk, BF16), V((8, 8) + blk, BF16),
        V((S, 128), F32), V((S, 128), F32),
        V((S, D // 2), F32), V((S, D // 2), BF16), V((S, D // 2), BF16), V((S, D // 2), BF16),
        V((16, 16, D // 2), BF16), V((8, 16, 128), BF16), V((8, 16, 128), BF16),
        pltpu.SemaphoreType.DMA((8,)),
        pltpu.SemaphoreType.DMA((N_GROUPS,)),
        pltpu.SemaphoreType.DMA((N_GROUPS,)),
    ]
    outs = pl.pallas_call(
        main_kernel,
        name="moe_exchange",
        out_shape=[
            V((2, D), F32), V((T, D), BF16), V(w_in.shape, BF16), V(w_out.shape, BF16),
        ],
        in_specs=[pl.BlockSpec(memory_space=pltpu.HBM)] * 5,
        out_specs=[pl.BlockSpec(memory_space=pltpu.VMEM)] * 4,
        scratch_shapes=scratch,
        compiler_params=pltpu.CompilerParams(
            collective_id=0, has_side_effects=True, vmem_limit_bytes=52 * 2**20
        ),
    )(tokens, slot_embed.reshape(2, 4, 2, 16, D), w_in, w_out, cotangent)
    embed_grad, token_grad, w_in_grad, w_out_grad = pl.pallas_call(
        write_kernel,
        name="write",
        out_shape=[shape((2, D), F32), shape((T, D), BF16), shape(w_in.shape, BF16), shape(w_out.shape, BF16)],
        in_specs=[pl.BlockSpec(memory_space=pltpu.VMEM)] * 4,
        out_specs=[pl.BlockSpec(memory_space=pl.ANY)] * 4,
        scratch_shapes=[pltpu.SemaphoreType.DMA((4,))],
        compiler_params=pltpu.CompilerParams(has_side_effects=True, vmem_limit_bytes=8 * 2**20),
    )(*outs)
    return (token_grad, embed_grad, w_in_grad, w_out_grad)


def solution(mesh):
    in_specs = (
        P(("seq", "expert"), None),
        P(),
        P("expert", None, "seq"),
        P("expert", "seq", None),
        P(("seq", "expert"), None),
    )
    out_specs = (
        P(("seq", "expert"), None),
        P(("seq", "expert"), None),
        P("expert", None, "seq"),
        P("expert", "seq", None),
    )
    return jax.shard_map(
        on_device, mesh=mesh, in_specs=in_specs, out_specs=out_specs, check_vma=False
    )
```

```python
import functools

import jax
import jax.numpy as jnp
from jax import lax
from jax.experimental import pallas as pl
from jax.experimental.pallas import tpu as pltpu
from jax.sharding import PartitionSpec as P

MESH = pl.DeviceIdType.MESH
F32 = jnp.float32
BF16 = jnp.bfloat16
CHUNK = 256
GELU_C = 0.7978845608028654
GELU_A = 0.044715


def coords():
    s = lax.axis_index("seq")
    e = lax.axis_index("expert")
    return s // 2, (s % 2) * 2 + e // 8, (e // 2) % 4, e % 2


def device(z, y, x, c):
    return (z * 2 + y // 2, (y % 2) * 8 + x * 2 + c)


def nn(a, b):
    return lax.dot_general(a, b, (((1,), (0,)), ((), ())), preferred_element_type=F32)


def nt(a, b):
    return lax.dot_general(a, b, (((1,), (1,)), ((), ())), preferred_element_type=F32)


def tn(a, b):
    return lax.dot_general(a, b, (((0,), (0,)), ((), ())), preferred_element_type=F32)


def hops(k):
    return min(k, 4 - k)


PLANE = sorted(
    ((a, b) for a in range(4) for b in range(4) if a or b), key=lambda p: -hops(p[0]) - hops(p[1])
)
RING = (2, 1, 3)


def rows_at(start, size, unit):
    return pl.ds(pl.multiple_of(start, unit), size)


def split3(v):
    hi = v.astype(BF16).astype(F32)
    mid = (v - hi).astype(BF16).astype(F32)
    lo = (v - hi - mid).astype(BF16).astype(F32)
    return hi, mid, lo


def scalar_tile(columns):
    parts = [p for v in columns for p in split3(v)]
    rows = columns[0].shape[0]
    lane = lax.broadcasted_iota(jnp.int32, (rows, 128), 1)
    tile = jnp.zeros((rows, 128), F32)
    for i, p in enumerate(parts):
        tile = jnp.where((lane >= 16 * i) & (lane < 16 * i + 16), p, tile)
    return tile


def scalar_of(tile, i):
    a = 48 * i
    return tile[:, a : a + 1] + tile[:, a + 16 : a + 17] + tile[:, a + 32 : a + 33]


def chunk_tiles(v16, z):
    h, q = z // 2, z % 2
    return [v16[8 * h : 8 * h + 8, 640 * q + 128 * j : 640 * q + 128 * j + 128] for j in range(5)]


def unpack_rows(blocks):
    out = []
    for j in range(10):
        q, jj = j // 5, j % 5
        out.append(
            jnp.concatenate([blocks[q][8 * jj : 8 * jj + 8], blocks[2 + q][8 * jj : 8 * jj + 8]], axis=0)
        )
    return out


class Group:
    def __init__(self, net, index, total):
        self.net, self.index, self.total = net, index, total

    def copy(self, src, dst, dev):
        return pltpu.make_async_remote_copy(
            src_ref=src, dst_ref=dst, send_sem=self.net.ss.at[self.index], recv_sem=self.net.rs.at[self.index],
            device_id=dev, device_id_type=MESH,
        )

    def put(self, src, dst, dev):
        self.copy(src, dst, dev).start()

    def wait_recv(self):
        self.copy(self.total, self.total, self.net.other).wait_recv()

    def wait_send(self):
        self.copy(self.total, self.total, self.net.other).wait_send()


class Net:
    def __init__(self, ss, rs, other):
        self.ss, self.rs, self.other, self.groups = ss, rs, other, []

    def group(self, total):
        g = Group(self, len(self.groups), total)
        self.groups.append(g)
        return g

    def put(self, src, dst, dev):
        g = self.group(dst)
        g.put(src, dst, dev)
        return g


N_GROUPS = 29
TILE0 = (8, 128)


def main_kernel(
    tok_h, emb_h, win_h, wout_h, cot_h,
    eg_o, tg_o, wi_o, wo_o,
    lhs, rhs, win_t, wout_t, tok_t, cot_t, p_s, r_s,
    tok, emb5, win, wout, cot,
    lt, et, cf, cb, m_s, s_s,
    u_own, u_cs, u_cr, u_xs, u_xr, u_pk, u_yr, sall,
    g_own, g_cs, g_cr, g_pk, g_zr, g_pk2, g_yr, gall,
    o_pk, o_sr, oall, i_pk, i_sr, iall,
    l_all, inner_all,
    c_own, c_cs, c_cr, c_ys, c_yr, c_xs, c_xr,
    ld, ss, rs,
):
    z, y, x, c = coords()
    ylo, yhi = y % 2, y // 2
    oc = 1 - c
    D = tok.shape[1]
    other = device(z, y, x, oc)
    net = Net(ss, rs, other)

    loads = {}

    def load(name, src, dst):
        cp = pltpu.make_async_copy(src, dst, ld.at[len(loads)])
        cp.start()
        loads[name] = cp

    for cc in range(2):
        for yy in range(2):
            pltpu.make_async_copy(emb_h.at[yy, :, cc], emb5.at[cc, :, yy], ld.at[0]).start()
    loads["emb"] = pltpu.make_async_copy(emb_h, emb5, ld.at[0])
    n_chunks = tok.shape[0] // CHUNK
    for t in range(n_chunks):
        load(("tok", t), tok_h.at[pl.ds(t * CHUNK, CHUNK)], tok.at[pl.ds(t * CHUNK, CHUNK)])
    load("cot", cot_h, cot)
    load("win", win_h, win)
    load("wout", wout_h, wout)

    barrier = pltpu.get_barrier_semaphore()
    partners = [(z, y, x, oc)]
    partners += [((z + a) % 4, (y + b) % 4, x, c) for a in range(4) for b in range(4) if a or b]
    partners += [(z, (y + b) % 4, (x + a) % 4, c) for a in range(1, 4) for b in range(4)]
    partners += [(z, y, (x + a) % 4, oc) for a in range(1, 4)]
    partners += [((z + a) % 4, y, (x + b) % 4, c) for a in range(1, 4) for b in range(1, 4)]
    for p in partners:
        pl.semaphore_signal(barrier, inc=1, device_id=device(*p), device_id_type=MESH)

    loads["emb"].wait()
    emb = emb5[...].reshape(-1, D)
    for t in range(n_chunks):
        loads[("tok", t)].wait()
        lt[:, t * CHUNK : (t + 1) * CHUNK] = nt(emb, tok[t * CHUNK : (t + 1) * CHUNK, :])

    ro = rows_at(oc * 128, 128, 128)
    rc = rows_at(c * 128, 128, 128)

    @pl.loop(0, n_chunks, unroll=4)
    def _(t):
        k = rows_at(t * CHUNK, CHUNK, CHUNK)
        l = lt[:, k]
        e = jnp.exp(l - jnp.max(l, axis=0, keepdims=True))
        f = e / jnp.sum(e, axis=0, keepdims=True)
        cf[:, k] = f
        cb[:, k] = f.astype(BF16)

    cot_load = loads["cot"]
    cot_load.wait()
    w_o = cb[ro, :]
    for n in range(D // 256):
        g_cs[:, n * 256 : (n + 1) * 256] = nn(w_o, cot[:, n * 256 : (n + 1) * 256]).astype(BF16)
    pl.semaphore_wait(barrier, len(partners))
    g_core = net.put(g_cs, g_cr, device(z, y, x, oc))

    @pl.loop(0, 8, unroll=8)
    def _(i):
        r = rows_at(i * 32, 32, 32)
        l = lt[r, :]
        m = jnp.max(l, axis=1, keepdims=True)
        e = jnp.exp(l - m)
        s = jnp.sum(e, axis=1, keepdims=True)
        et[r, :] = e.astype(BF16)
        m_s[r, :] = jnp.broadcast_to(m, (32, 128))
        s_s[r, :] = jnp.broadcast_to(s, (32, 128))

    w_o = et[ro, :]
    for n in range(D // 256):
        u_cs[:, n * 256 : (n + 1) * 256] = nn(w_o, tok[:, n * 256 : (n + 1) * 256]).astype(BF16)
    u_cs[:, D : D + 128] = scalar_tile([m_s[ro, 0:1], s_s[ro, 0:1]]).astype(BF16)
    u_core = net.put(u_cs, u_cr, device(z, y, x, oc))
    w_c = cb[rc, :]
    for n in range(D // 256):
        g_own[:, n * 256 : (n + 1) * 256] = nn(w_c, cot[:, n * 256 : (n + 1) * 256])
    g_core.wait_recv()

    @pl.loop(0, 4, unroll=2)
    def _(i):
        r = rows_at(i * 32, 32, 32)
        v = g_own[r, :] + g_cr[r, :].astype(F32)
        for zz in range(4):
            tiles = chunk_tiles(v[:16], zz) + chunk_tiles(v[16:], zz)
            g_pk[zz, rows_at(i * 80, 80, 16), :] = jnp.concatenate(tiles, axis=0).astype(BF16)

    g_z = net.group(g_zr)
    for k in RING:
        zz = (z + k) % 4
        g_z.put(g_pk.at[zz], g_zr.at[k - 1], device(zz, y, x, c))

    w_c = et[rc, :]
    for n in range(D // 256):
        u_own[:, n * 256 : (n + 1) * 256] = nn(w_c, tok[:, n * 256 : (n + 1) * 256])

    u_core.wait_recv()

    def merge_core(first):
        r = rows_at(first, 16, 16)
        rg = rows_at(c * 128 + first, 16, 16)
        v = u_cr[r, :].astype(F32)
        m1, s1 = m_s[rg, 0:1], s_s[rg, 0:1]
        sc = v[:, D : D + 128]
        m2, s2 = scalar_of(sc, 0), scalar_of(sc, 1)
        m = jnp.maximum(m1, m2)
        f1, f2 = jnp.exp(m1 - m), jnp.exp(m2 - m)
        s = s1 * f1 + s2 * f2
        u = u_own[r, :] * f1 + v[:, :D] * f2
        u_own[r, :] = u
        u_xs[r, :] = jnp.concatenate([u, scalar_tile([m, s])], axis=1).astype(BF16)
        m_s[rg, :] = jnp.broadcast_to(m, (16, 128))
        s_s[rg, :] = jnp.broadcast_to(s, (16, 128))

    u_x = net.group(u_xr)
    for k in RING + (0,):
        xx = (x + k) % 4
        merge_core(xx * 32)
        merge_core(xx * 32 + 16)
        if k:
            u_x.put(u_xs.at[rows_at(xx * 32, 32, 32)], u_xr.at[k - 1], device(z, y, xx, c))

    loads["win"].wait()
    loads["wout"].wait()
    for e in range(4):
        wout_t[e] = wout[e].T
        win_t[e] = win[e].T

    g_z.wait_recv()

    @pl.loop(0, 4, unroll=2)
    def _(i):
        r = rows_at(i * 80, 80, 16)
        v = g_pk[z, r, :].astype(F32)
        for k in range(3):
            v = v + g_zr[k, r, :].astype(F32)
        pad = jnp.zeros(TILE0, F32)
        g_pk2[2 * i] = jnp.concatenate([v[:40], pad], axis=0).astype(BF16)
        g_pk2[2 * i + 1] = jnp.concatenate([v[40:], pad], axis=0).astype(BF16)

    g_xy = net.group(g_yr.at[pl.ds(1, 15)])
    for a, b in PLANE:
        xx, yy = (x + a) % 4, (y + b) % 4
        g_xy.put(g_pk2.at[xx * 2 + yy % 2], g_yr.at[a * 4 + b], device(z, yy, xx, c))
    g_yr[0] = g_pk2[x * 2 + ylo]

    u_x.wait_recv()
    for yy in range(2):
        r0 = x * 32 + yy * 16
        r = rows_at(r0, 16, 16)
        rg = rows_at(c * 128 + r0, 16, 16)
        ms, sums, us = [m_s[rg, 0:1]], [s_s[rg, 0:1]], [u_own[r, :]]
        for k in range(3):
            v = u_xr[k, yy * 16 : yy * 16 + 16, :].astype(F32)
            sc = v[:, D : D + 128]
            ms.append(scalar_of(sc, 0))
            sums.append(scalar_of(sc, 1))
            us.append(v[:, :D])
        m = functools.reduce(jnp.maximum, ms)
        fs = [jnp.exp(mk - m) for mk in ms]
        s = sum(a * f for a, f in zip(sums, fs))
        u = sum(a * f for a, f in zip(us, fs))
        tile = scalar_tile([m, s])
        for zz in range(4):
            h = zz // 2
            tiles = chunk_tiles(u, zz) + [tile[8 * h : 8 * h + 8]]
            u_pk[yy * 4 + zz] = jnp.concatenate(tiles, axis=0).astype(BF16)
    u_yz = net.group(u_yr.at[pl.ds(1, 15)])
    for a, b in PLANE:
        zz, yy = (z + a) % 4, (y + b) % 4
        u_yz.put(u_pk.at[(yy % 2) * 4 + zz], u_yr.at[a * 4 + b], device(zz, yy, x, c))
    u_yr[0] = u_pk[ylo * 4 + z]

    for t in range(n_chunks):
        k = pl.ds(t * CHUNK, CHUNK)
        tok_t[:, k] = tok[k, :].T
        cot_t[:, k] = cot[k, :].T

    g_xy.wait_recv()
    acc = g_yr[0].astype(F32)
    for k in range(1, 16):
        acc = acc + g_yr[k].astype(F32)
    gall[z] = acc.astype(BF16)
    g_ag = net.group(gall.at[pl.ds(0, 3)])
    for k in RING:
        g_ag.put(gall.at[z], gall.at[z], device((z + k) % 4, y, x, c))

    u_yz.wait_recv()
    parts = [u_yr[k].astype(F32) for k in range(16)]
    ms = [scalar_of(v[40:48], 0) for v in parts]
    sums = [scalar_of(v[40:48], 1) for v in parts]
    m = functools.reduce(jnp.maximum, ms)
    fs = [jnp.exp(mk - m) for mk in ms]
    s = sum(a * f for a, f in zip(sums, fs))
    lse = m + jnp.log(s)
    lse_tile = scalar_tile([lse])
    tiles = []
    for j in range(5):
        tiles.append(sum(v[8 * j : 8 * j + 8] * f for v, f in zip(parts, fs)) / s)
    sall[z] = jnp.concatenate(tiles + [lse_tile], axis=0).astype(BF16)
    u_ag = net.group(sall.at[pl.ds(0, 3)])
    for k in RING:
        u_ag.put(sall.at[z], sall.at[z], device((z + k) % 4, y, x, c))

    def seq_sums(pk, sr, by_z):
        group = net.group(sr.at[pl.ds(1, 15)])
        for a, b in PLANE:
            zz, yy = (z + a) % 4, (y + b) % 4
            group.put(pk.at[zz if by_z else yy], sr.at[a * 4 + b], device(zz, yy, x, c))
        sr[0] = pk[z if by_z else y]
        return group

    def seq_total(sr, parity, rows):
        ks = [a * 4 + b for a in range(4) for b in range(4) if b % 2 == parity]
        acc = sr[ks[0]].astype(F32)[:rows]
        for k in ks[1:]:
            acc = acc + sr[k].astype(F32)[:rows]
        return acc

    F = win.shape[2]
    expert_of = lax.broadcasted_iota(jnp.int32, (16, 1), 0) // 4
    g_ag.wait_recv()
    slot_grad = jnp.concatenate(unpack_rows([gall[k].astype(F32) for k in range(4)]), axis=1).astype(BF16)
    hid_grad = jnp.zeros((16, F), F32)
    for e in range(4):
        hid_grad = jnp.where(expert_of == e, nn(slot_grad, wout_t[e]), hid_grad)
    u_ag.wait_recv()
    slot_in_f = jnp.concatenate(unpack_rows([sall[k].astype(F32) for k in range(4)]), axis=1)
    slot_in = slot_in_f.astype(BF16)
    pre = jnp.zeros((16, F), F32)
    hidden_f = jnp.zeros((16, F), F32)
    pre_grad = jnp.zeros((16, F), F32)
    out_part = jnp.zeros((16, D), F32)
    for e in range(4):
        own = expert_of == e
        v = nn(slot_in, win[e])
        th = jnp.tanh(GELU_C * (v + GELU_A * v * v * v))
        act = jnp.where(own, 0.5 * v * (1.0 + th), 0.0)
        slope = 0.5 * (1.0 + th) + 0.5 * v * (1.0 - th * th) * GELU_C * (1.0 + 3.0 * GELU_A * v * v)
        out_part += nn(act.astype(BF16), wout[e])
        hidden_f += act
        pre = jnp.where(own, v, pre)
        pre_grad += jnp.where(own, hid_grad * slope, 0.0)
    for zz in range(4):
        tile = sall[zz].astype(F32)[40:48]
        o_pk[zz] = jnp.concatenate(chunk_tiles(out_part, zz) + [tile], axis=0).astype(BF16)
    o_seq = seq_sums(o_pk, o_sr, True)
    in_part = jnp.zeros((16, D), F32)
    for e in range(4):
        in_part += nn(jnp.where(expert_of == e, pre_grad, 0.0).astype(BF16), win_t[e])
    pre_grad = pre_grad.astype(BF16)
    inner_part = jnp.sum(pre * pre_grad.astype(F32), axis=1, keepdims=True)
    tile = scalar_tile([inner_part])
    for zz in range(4):
        h = zz // 2
        tiles = chunk_tiles(in_part, zz) + [tile[8 * h : 8 * h + 8]]
        i_pk[zz] = jnp.concatenate(tiles, axis=0).astype(BF16)
    i_seq = seq_sums(i_pk, i_sr, False)

    for e in range(4):
        own = expert_of == e
        wo_o[e] = tn(jnp.where(own, hidden_f, 0.0).astype(BF16), slot_grad).astype(BF16)
        wi_o[e] = tn(jnp.where(own, slot_in_f, 0.0).astype(BF16), pre_grad).astype(BF16)

    o_seq.wait_recv()
    pair = c * 8 + x * 2
    for parity in range(2):
        acc = seq_total(o_sr, parity, 40)
        lse_tile = o_sr[parity].astype(F32)[40:48]
        oall[pair + (ylo + parity) % 2, z] = jnp.concatenate([acc, lse_tile], axis=0).astype(BF16)
    o_all = [net.group(oall.at[pl.ds(0, 2), pl.ds(0, 3)])] + [net.group(oall.at[pl.ds(0, 2)]) for _ in range(3)]
    ref = oall.at[pl.ds(pair, 2), z]
    for k, a in PLANE:
        o_all[k].put(ref, ref, device((z + a) % 4, y, (x + k) % 4, c))

    i_seq.wait_recv()
    cy = c * 4 + y
    for parity in range(2):
        acc = seq_total(i_sr, parity, 48)
        inner = scalar_of(acc[40:48], 0)
        block = jnp.concatenate([acc[:40], scalar_tile([inner])], axis=0)
        iall[cy, x * 2 + (ylo + parity) % 2] = block.astype(BF16)
    i_all = [net.group(iall.at[0, pl.ds(0, 6)])] + [net.group(iall.at[0]) for _ in range(3)]
    ref = iall.at[cy, pl.ds(x * 2, 2)]
    for k, a in PLANE:
        i_all[k].put(ref, ref, device(z, (y + k) % 4, (x + a) % 4, c))

    half = rhs.shape[0] // 2

    def place(i, blocks, scalars):
        r = rows_at(i * 16, 16, 16)
        for j, t in enumerate(unpack_rows(blocks)):
            rhs[r, j * 128 : (j + 1) * 128] = t.astype(BF16)
        v = jnp.concatenate([scalar_of(blocks[0][40:48], 0), scalar_of(blocks[2][40:48], 0)], axis=0)
        scalars[r, :] = jnp.broadcast_to(v, (16, 128))

    def place_out(first):
        for i in range(2):
            place(first + i, [oall[first + i, k].astype(F32) for k in range(4)], l_all)

    def place_in(core):
        @pl.loop(0, 8, unroll=8)
        def _(k):
            place(core * 8 + k, [iall[core * 4 + zz, k].astype(F32) for zz in range(4)], inner_all)

    o_3, i_3 = [], []
    for k in range(4):
        o_all[k].wait_recv()
        ref = oall.at[pl.ds(c * 8 + ((x - k + 4) % 4) * 2, 2)]
        o_3.append(net.put(ref, ref, other))
    for k in range(4):
        place_out(c * 8 + k * 2)

    def comb(core, first):
        rows = rows_at(core * 128, 128, 128)
        for t in range(n_chunks):
            k = pl.ds(t * CHUNK, CHUNK)
            p = cf[rows, k] * nn(rhs[rows, :], cot_t[:, k])
            total = jnp.sum(p, axis=0, keepdims=True)
            p_s[rows, k] = p
            r_s[:, k] = total if first else r_s[:, k] + total
            df = jnp.exp(lt[rows, k] - l_all[rows, 0:1])
            lt[rows, k] = df
            lhs[rows, k] = df.astype(BF16)

    comb(c, True)
    for k in range(4):
        i_all[k].wait_recv()
        ref = iall.at[c * 4 + (y - k + 4) % 4]
        i_3.append(net.put(ref, ref, other))
    for k in range(4):
        o_3[k].wait_recv()
    for k in range(4):
        place_out(oc * 8 + k * 2)
    comb(oc, False)

    H = D // 2
    pieces = ((0, 384), (384, 256))
    c_core = net.group(c_cr)

    def tail(core):
        place_in(core)
        rows = rows_at(core * 128, 128, 128)
        rows_g = rows_at(half + core * 128, 128, 128)
        for t in range(n_chunks):
            k = pl.ds(t * CHUNK, CHUNK)
            dg = nn(rhs[rows, :], tok_t[:, k])
            lc = p_s[rows, k] - cf[rows, k] * r_s[:, k]
            lhs[rows_g, k] = (lt[rows, k] * (dg - inner_all[rows, 0:1]) + lc).astype(BF16)
        w = lhs[rows_g, :]
        for a, b in pieces:
            c_cs[rows, a : a + b] = nn(w, tok[:, rows_at(oc * H + a, b, 128)]).astype(BF16)
        c_core.put(c_cs.at[rows], c_cr.at[rows], other)
        for a, b in pieces:
            c_own[rows, a : a + b] = nn(w, tok[:, rows_at(c * H + a, b, 128)])

    tail(c)
    for cp in i_3:
        cp.wait_recv()
    tail(oc)
    c_core.wait_recv()

    @pl.loop(0, 16, unroll=4)
    def _(i):
        r = rows_at(i * 16, 16, 16)
        c_ys[r, :] = (c_own[r, :] + c_cr[r, :].astype(F32)).astype(BF16)

    def block_of(zz, yy):
        return rows_at((yy % 2) * 128 + ((zz % 2) * 2 + yy // 2) * 32 + (zz // 2) * 16, 16, 16)

    c_y = net.group(c_yr.at[pl.ds(1, 15)])
    for a, b in PLANE:
        zz, yy = (z + a) % 4, (y + b) % 4
        c_y.put(c_ys.at[block_of(zz, yy)], c_yr.at[a * 4 + b], device(zz, yy, x, c))
    c_yr[0] = c_ys[block_of(z, y), :]
    rhs[half:, :] = emb5[...].reshape(-1, D)
    for t in range(n_chunks):
        k = pl.ds(t * CHUNK, CHUNK)
        tg_o[k, :] = tn(lhs[:, k], rhs[...]).astype(BF16)
    c_y.wait_recv()
    acc = c_yr[0].astype(F32)
    for k in range(1, 16):
        acc = acc + c_yr[k].astype(F32)
    blocks = H // 128
    at = lax.broadcasted_iota(jnp.int32, (128, 16 * blocks), 0)
    of = lax.broadcasted_iota(jnp.int32, (128, 16 * blocks), 1)
    t_of, r_of = of // 16, of % 16
    pick = at == (r_of // 2) * 16 + 2 * t_of + r_of % 2
    stacked = jnp.concatenate([acc[:, 128 * t : 128 * t + 128] for t in range(blocks)], axis=0).astype(BF16)
    packed = nn(jnp.where(pick, 1.0, 0.0).astype(BF16), stacked)
    for j in range(8):
        c_xs[j] = packed[16 * j : 16 * j + 16].astype(BF16)
    c_x = net.group(c_xr.at[pl.ds(1, 7)])
    for k in RING + (0,):
        for d in range(2):
            if k or d:
                xx, cc = (x + k) % 4, c if d == 0 else oc
                c_x.put(c_xs.at[xx * 2 + cc], c_xr.at[k * 2 + d], device(z, y, xx, cc))
    c_xr[0] = c_xs[x * 2 + c]
    c_x.wait_recv()
    for d in range(2):
        v = sum(c_xr[2 * k + d].astype(F32) for k in range(4))
        out = jnp.concatenate([v[2 * t : 2 * t + 2] for t in range(blocks)], axis=1)
        eg_o[:, rows_at((c if d == 0 else oc) * H, H, 128)] = out

    for g in net.groups:
        g.wait_send()


def write_kernel(eg, tg, wi, wo, eg_h, tg_h, wi_h, wo_h, sem):
    copies = [
        pltpu.make_async_copy(src, dst, sem.at[i])
        for i, (src, dst) in enumerate(((eg, eg_h), (wi, wi_h), (wo, wo_h), (tg, tg_h)))
    ]
    for cp in copies:
        cp.start()
    for cp in copies:
        cp.wait()


def on_device(tokens, slot_embed, w_in, w_out, cotangent):
    T, D = tokens.shape
    S = slot_embed.shape[0]
    E, _, F = w_in.shape
    V = pltpu.VMEM
    shape = jax.ShapeDtypeStruct
    blk = (48, 128)
    scratch = [
        V((2 * S, T), BF16), V((2 * S, D), BF16),
        V((E, F, D), BF16), V((E, D, F), BF16), V((D, T), BF16), V((D, T), BF16), V((S, T), F32), V((1, T), F32),
        V((T, D), BF16), V((2, 4, 2, 16, D), BF16), V(w_in.shape, BF16), V(w_out.shape, BF16), V((T, D), BF16),
        V((S, T), F32), V((S, T), BF16), V((S, T), F32), V((S, T), BF16), V((S, 128), F32), V((S, 128), F32),
        V((128, D), F32), V((128, D + 128), BF16), V((128, D + 128), BF16),
        V((128, D + 128), BF16), V((3, 32, D + 128), BF16), V((8,) + blk, BF16), V((16,) + blk, BF16), V((4,) + blk, BF16),
        V((128, D), F32), V((128, D), BF16), V((128, D), BF16), V((4, 320, 128), BF16), V((3, 320, 128), BF16),
        V((8,) + blk, BF16), V((16,) + blk, BF16), V((4,) + blk, BF16),
        V((4,) + blk, BF16), V((16,) + blk, BF16), V((16, 4) + blk, BF16),
        V((4,) + blk, BF16), V((16,) + blk, BF16), V((8, 8) + blk, BF16),
        V((S, 128), F32), V((S, 128), F32),
        V((S, D // 2), F32), V((S, D // 2), BF16), V((S, D // 2), BF16), V((S, D // 2), BF16),
        V((16, 16, D // 2), BF16), V((8, 16, 128), BF16), V((8, 16, 128), BF16),
        pltpu.SemaphoreType.DMA((8,)),
        pltpu.SemaphoreType.DMA((N_GROUPS,)),
        pltpu.SemaphoreType.DMA((N_GROUPS,)),
    ]
    outs = pl.pallas_call(
        main_kernel,
        name="moe_exchange",
        out_shape=[
            V((2, D), F32), V((T, D), BF16), V(w_in.shape, BF16), V(w_out.shape, BF16),
        ],
        in_specs=[pl.BlockSpec(memory_space=pltpu.HBM)] * 5,
        out_specs=[pl.BlockSpec(memory_space=pltpu.VMEM)] * 4,
        scratch_shapes=scratch,
        compiler_params=pltpu.CompilerParams(
            collective_id=0, has_side_effects=True, vmem_limit_bytes=52 * 2**20
        ),
    )(tokens, slot_embed.reshape(2, 4, 2, 16, D), w_in, w_out, cotangent)
    embed_grad, token_grad, w_in_grad, w_out_grad = pl.pallas_call(
        write_kernel,
        name="write",
        out_shape=[shape((2, D), F32), shape((T, D), BF16), shape(w_in.shape, BF16), shape(w_out.shape, BF16)],
        in_specs=[pl.BlockSpec(memory_space=pltpu.VMEM)] * 4,
        out_specs=[pl.BlockSpec(memory_space=pl.ANY)] * 4,
        scratch_shapes=[pltpu.SemaphoreType.DMA((4,))],
        compiler_params=pltpu.CompilerParams(has_side_effects=True, vmem_limit_bytes=8 * 2**20),
    )(*outs)
    return (token_grad, embed_grad, w_in_grad, w_out_grad)


def solution(mesh):
    in_specs = (
        P(("seq", "expert"), None),
        P(),
        P("expert", None, "seq"),
        P("expert", "seq", None),
        P(("seq", "expert"), None),
    )
    out_specs = (
        P(("seq", "expert"), None),
        P(("seq", "expert"), None),
        P("expert", None, "seq"),
        P("expert", "seq", None),
    )
    return jax.shard_map(
        on_device, mesh=mesh, in_specs=in_specs, out_specs=out_specs, check_vma=False
    )
```
